32 devices in a mesh: px: 4 (over x, core), py: 8 (over z, y).
Axes of the slice: x: 2, y: 2, z: 4, core: 2. Of those that a mesh axis runs over, the one named last changes fastest.
Arguments:
- field: float32 [5, 32, 128, 128], P(None, 'px', 'py'), may hold values from -6 to 6
- forcing: float32 [5, 32, 128, 128], P(None, 'px', 'py'), may hold values from -6 to 6
- x_inverse: float32 [5, 5, 32, 128, 128], P(None, None, 'px', 'py'), may hold values from -1 to 1
- x_lower: float32 [5, 5, 32, 128, 128], P(None, None, 'px', 'py'), may hold values from -1 to 1
- x_upper: float32 [5, 5, 32, 128, 128], P(None, None, 'px', 'py'), may hold values from -1 to 1
- y_inverse: float32 [5, 5, 32, 128, 128], P(None, None, 'px', 'py'), may hold values from -1 to 1
- y_lower: float32 [5, 5, 32, 128, 128], P(None, None, 'px', 'py'), may hold values from -1 to 1
- y_upper: float32 [5, 5, 32, 128, 128], P(None, None, 'px', 'py'), may hold values from -1 to 1
Outputs:
- update: float32 [5, 32, 128, 128], P(None, 'px', 'py')
The draws below stay inside these ranges and needn't reach their ends.
All inputs are finite; a program needn't handle non-finite values.
Results may differ from the reference program's by a relative error of at most 0.00014.
Values sent between devices are 32-bit elements; how exact they have to be, the bound alone decides.
No kernel may reach another device: no remote copies, remote signals or barrier semaphores. Data moves between devices by JAX's collectives and lax.ppermute only.
A program may use at most 64 MiB of HBM per device.

```python
import math
import jax
import jax.numpy as jnp
from jax import lax

NVAR = 5
NX = 32
NY = 128
NZ = 128


def coupling_block(key, line_dim, cells_per_line):
    array_extent = (NX, NY, NZ)
    line_shape = tuple((1 if k == line_dim else array_extent[k] for k in range(3)))
    random_keys = jax.random.split(key, 8)
    slow_share = 0.5
    slow = jax.random.bernoulli(random_keys[0], slow_share, (1,) + line_shape)
    spread = jnp.exp(jax.random.uniform(random_keys[1], (NVAR,) + array_extent, jnp.float32, math.log(0.6), math.log(1.6)))
    decay_rate = jnp.where(slow, 0.5 / cells_per_line, 3.0 / 40.0) * spread
    message_group = jax.random.bernoulli(random_keys[2], 3.0 / cells_per_line, (1,) + array_extent)
    damping_terms = jax.random.uniform(random_keys[3], (NVAR,) + array_extent, jnp.float32, 0.5, 0.8)
    retained_part = jnp.exp(-decay_rate) * jnp.where(message_group, damping_terms, 1.0)
    signs = jnp.where(jax.random.bernoulli(random_keys[5], 0.5, (2,) + array_extent), 1.0, -1.0)
    angles = jax.random.uniform(random_keys[4], (2,) + array_extent, jnp.float32, 0.4, 1.0) * signs
    cosine = jnp.cos(angles)
    sine = jnp.sin(angles)
    reflect_signs = jnp.where(jax.random.bernoulli(random_keys[6], 0.5, (NVAR,) + array_extent), 1.0, -1.0)
    reflect_axis = jax.random.uniform(random_keys[7], (NVAR,) + array_extent, jnp.float32, 0.5, 1.5) * reflect_signs
    norm_squared = jnp.sum(reflect_axis * reflect_axis, axis=0)
    unit_matrix = jnp.eye(NVAR, dtype=jnp.float32)[:, :, None, None, None]
    reflection = unit_matrix - 2.0 * reflect_axis[:, None] * reflect_axis[None, :] / norm_squared
    rows = [cosine[0] * reflection[0] - sine[0] * reflection[1], sine[0] * reflection[0] + cosine[0] * reflection[1], cosine[1] * reflection[2] - sine[1] * reflection[3], sine[1] * reflection[2] + cosine[1] * reflection[3], reflection[4]]
    matrix = jnp.stack(rows)
    return (retained_part[:, None] * matrix).astype(jnp.float32)


def inverse_block(key, cells_per_line):
    array_extent = (NX, NY, NZ)
    random_keys = jax.random.split(key, 2)
    lowest, highest = (0.5, 1.5)
    scales = jnp.exp(jax.random.uniform(random_keys[0], (NVAR, 1) + array_extent, jnp.float32, math.log(lowest), math.log(highest)))
    scales = scales * float(cells_per_line) ** (-0.75)
    mixing = jax.random.uniform(random_keys[1], (NVAR, NVAR) + array_extent, jnp.float32, -0.2, 0.2)
    unit_matrix = jnp.eye(NVAR, dtype=jnp.float32)[:, :, None, None, None]
    return (scales * (unit_matrix + mixing * (1.0 - unit_matrix))).astype(jnp.float32)


def draw_x_inverse(key, part):
    return inverse_block(jax.random.fold_in(key, 101), NX)


def draw_x_lower(key, part):
    return coupling_block(jax.random.fold_in(key, 102), 0, NX)


def draw_x_upper(key, part):
    return coupling_block(jax.random.fold_in(key, 103), 0, NX)


def draw_y_inverse(key, part):
    return inverse_block(jax.random.fold_in(key, 104), NY)


def draw_y_lower(key, part):
    return coupling_block(jax.random.fold_in(key, 105), 1, NY)


def draw_y_upper(key, part):
    return coupling_block(jax.random.fold_in(key, 106), 1, NY)


def level_of(rng, extent, shards, low, largest):
    gain, own = 1.0, jax.random.fold_in(rng, 6)
    for axis_at, parts in shards:
        draws = jnp.exp(jax.random.uniform(jax.random.fold_in(own, axis_at), (parts,), jnp.float32, low / len(shards), largest / len(shards)))
        gain = gain * jnp.repeat(draws, extent[axis_at] // parts).reshape([-1 if axis == axis_at else 1 for axis in range(len(extent))])
    return gain


def scatter_about(key, shape, deviation, most, cuts=(), kind=jnp.bfloat16):
    values = deviation * jax.random.normal(key, shape, jnp.float32)
    if cuts:
        values = values * level_of(key, shape, cuts, -0.22, 0.18)
    return jnp.clip(values, -most, most).astype(kind)


def setup_inputs(seed: int = 0) -> dict:
    streams_of = jax.random.split(jax.random.key(seed), 9)
    return {
        "field": scatter_about(streams_of[0], (NVAR, NX, NY, NZ), 1.0, 6.0, ((1, 4), (2, 8)), jnp.float32),
        "forcing": scatter_about(streams_of[1], (NVAR, NX, NY, NZ), 1.0, 6.0, ((1, 4), (2, 8)), jnp.float32),
        "x_inverse": draw_x_inverse(jax.random.fold_in(streams_of[8], 71), 0),
        "x_lower": draw_x_lower(jax.random.fold_in(streams_of[8], 71), 0),
        "x_upper": draw_x_upper(jax.random.fold_in(streams_of[8], 71), 0),
        "y_inverse": draw_y_inverse(jax.random.fold_in(streams_of[8], 71), 0),
        "y_lower": draw_y_lower(jax.random.fold_in(streams_of[8], 71), 0),
        "y_upper": draw_y_upper(jax.random.fold_in(streams_of[8], 71), 0),
    }


DISSIPATION = 0.1


def apply_block(blocks, vector):
    return jnp.sum(blocks * vector[None], axis=1)


def fourth_diff(values, line_axis):
    length = values.shape[line_axis]
    widths = [(0, 0)] * values.ndim
    widths[line_axis] = (2, 2)
    padded = jnp.pad(values, widths)

    def window(k):
        return lax.slice_in_dim(padded, k, k + length, axis=line_axis)

    return window(0) - 4.0 * window(1) + 6.0 * window(2) - 4.0 * window(3) + window(4)


def run_cells(source, coupling, inflow, line_axis, backward):
    length = source.shape[line_axis]

    def advance(i, carried):
        before, result = carried
        k = length - 1 - i if backward else i
        here = lax.dynamic_index_in_dim(coupling, k, line_axis + 1, keepdims=False)
        current = lax.dynamic_index_in_dim(source, k, line_axis, keepdims=False) - apply_block(here, before)
        return current, lax.dynamic_update_index_in_dim(result, current, k, line_axis)

    return lax.fori_loop(0, length, advance, (inflow, jnp.zeros_like(source)))[1]


def line_sweep(rhs, inverse, lower, upper, line_axis):
    source = apply_block(inverse, rhs)
    start = jnp.zeros(rhs.shape[:line_axis] + rhs.shape[line_axis + 1:], rhs.dtype)
    forward = run_cells(source, lower, start, line_axis, False)
    return run_cells(forward, upper, start, line_axis, True)


def reference(field, forcing, x_inverse, x_lower, x_upper, y_inverse, y_lower, y_upper):
    rhs = forcing - DISSIPATION * (fourth_diff(field, 1) + fourth_diff(field, 2))
    x_result = line_sweep(rhs, x_inverse, x_lower, x_upper, 1)
    return line_sweep(x_result, y_inverse, y_lower, y_upper, 2)
```

```python
import functools

import jax
import jax.numpy as jnp
from jax import lax
from jax.experimental import pallas as pl
from jax.experimental.pallas import tpu as pltpu
from jax.sharding import PartitionSpec as P

DISSIPATION = 0.1
NVAR = 5
F32 = jnp.float32
ROWS = 8
VMEM_BYTES = 56 * 1024 * 1024


def call(kernel, name, out_shapes, scratch=()):
    shapes = [jax.ShapeDtypeStruct(s, F32) for s in out_shapes]
    single = len(shapes) == 1
    return pl.pallas_call(
        kernel,
        name=name,
        out_shape=shapes[0] if single else shapes,
        scratch_shapes=[pltpu.VMEM(s, F32) for s in scratch],
        compiler_params=pltpu.CompilerParams(vmem_limit_bytes=VMEM_BYTES),
    )


def tree(terms):
    while len(terms) > 1:
        pairs = [terms[k] + terms[k + 1] for k in range(0, len(terms) - 1, 2)]
        terms = pairs + (terms[-1:] if len(terms) % 2 else [])
    return terms[0]


def matvec(load, vector):
    return [tree([load(a, b) * vector[b] for b in range(NVAR)]) for a in range(NVAR)]


def matmat(load, matrix):
    out = []
    for a in range(NVAR):
        row = [load(a, b) for b in range(NVAR)]
        for c in range(NVAR):
            out.append(tree([row[b] * matrix[NVAR * b + c] for b in range(NVAR)]))
    return out


def plus(left, right):
    return [p + q for p, q in zip(left, right, strict=True)]


def minus(left, right):
    return [p - q for p, q in zip(left, right, strict=True)]


def compose_lines(length, lower_at, upper_at, store_p, load_p, emit):
    first = [-lower_at(0, a, b) for a in range(NVAR) for b in range(NVAR)]
    store_p(0, first)

    def forward(i, p):
        p = [-q for q in matmat(lambda a, b: lower_at(i, a, b), p)]
        store_p(i, p)
        return tuple(p)

    last = lax.fori_loop(1, length, forward, tuple(first))
    emit(0, last)

    def backward(k, carried):
        w, r = carried
        i = length - 1 - k
        at = lambda a, b: upper_at(i, a, b)
        w = minus(load_p(i), matmat(at, list(w)))
        r = [-q for q in matmat(at, list(r))]
        return tuple(w), tuple(r)

    r = tuple(-upper_at(length - 1, a, b) for a in range(NVAR) for b in range(NVAR))
    w, r = lax.fori_loop(1, length, backward, (last, r))
    emit(1, r)
    emit(2, w)


def compose_x_kernel(lower, upper, out, held):
    cells, rows = lower.shape[2], lower.shape[3]

    def group(g, _):
        here = pl.ds(pl.multiple_of(g * ROWS, ROWS), ROWS)

        def emit(which, matrix):
            for a in range(NVAR):
                for b in range(NVAR):
                    out[which, a, b, here] = matrix[NVAR * a + b]

        def store_p(i, p):
            for k in range(NVAR * NVAR):
                held[i, k] = p[k]

        compose_lines(
            cells,
            lambda i, a, b: lower[a, b, i, here],
            lambda i, a, b: upper[a, b, i, here],
            store_p,
            lambda i: [held[i, k] for k in range(NVAR * NVAR)],
            emit,
        )
        return 0

    lax.fori_loop(0, rows // ROWS, group, 0)


def compose_y_kernel(cells_x, cells_y, lower, upper, out, held):
    def emit(which, matrix):
        for a in range(NVAR):
            for b in range(NVAR):
                out[which, a, b] = matrix[NVAR * a + b]

    def store_p(i, p):
        for k in range(NVAR * NVAR):
            held[i, k] = p[k]

    compose_lines(
        cells_y,
        lambda j, a, b: lower[a, b, pl.ds(j, cells_x, stride=cells_y), :],
        lambda j, a, b: upper[a, b, pl.ds(j, cells_x, stride=cells_y), :],
        store_p,
        lambda i: [held[i, k] for k in range(NVAR * NVAR)],
        emit,
    )


def local_x_kernel(
    field, forcing, x_before, x_after, y_before, y_after, inverse, lower, upper,
    reduced, source_out, padded, held,
):
    cells, rows, lanes = field.shape[1:]
    zero = jnp.zeros((rows, lanes), F32)
    middle = pl.ds(ROWS, rows)
    for c in range(NVAR):
        for i in range(cells):
            padded[c, i + 2, middle] = field[c, i]
            padded[c, i + 2, ROWS - 2 : ROWS] = y_before[c, i]
            padded[c, i + 2, ROWS + rows : ROWS + rows + 2] = y_after[c, i]
        for k in range(2):
            padded[c, k, middle] = x_before[c, k]
            padded[c, cells + 2 + k, middle] = x_after[c, k]

    def right_side(i):
        out = []
        for c in range(NVAR):
            centre = padded[c, i + 2, middle]
            along_x = (
                padded[c, i, middle] - 4.0 * padded[c, i + 1, middle] + 6.0 * centre
                - 4.0 * padded[c, i + 3, middle] + padded[c, i + 4, middle]
            )
            along_y = (
                padded[c, i + 2, pl.ds(ROWS - 2, rows)]
                - 4.0 * padded[c, i + 2, pl.ds(ROWS - 1, rows)]
                + 6.0 * centre
                - 4.0 * padded[c, i + 2, pl.ds(ROWS + 1, rows)]
                + padded[c, i + 2, pl.ds(ROWS + 2, rows)]
            )
            out.append(forcing[c, i] - DISSIPATION * (along_x + along_y))
        return out

    def forward(i, v):
        s = matvec(lambda a, b: inverse[a, b, i], right_side(i))
        for c in range(NVAR):
            source_out[c, i] = s[c]
        v = minus(s, matvec(lambda a, b: lower[a, b, i], list(v)))
        for c in range(NVAR):
            held[c, i] = v[c]
        return tuple(v)

    v = lax.fori_loop(0, cells, forward, (zero,) * NVAR)
    for c in range(NVAR):
        reduced[0, c] = v[c]

    def backward(k, w):
        i = cells - 1 - k
        product = matvec(lambda a, b: upper[a, b, i], list(w))
        return tuple(held[c, i] - product[c] for c in range(NVAR))

    w = lax.fori_loop(0, cells, backward, (zero,) * NVAR)
    for c in range(NVAR):
        reduced[1, c] = w[c]


def vec(ref, which):
    return [ref[which, c] for c in range(NVAR)]


def block(ref, which):
    return lambda a, b: ref[which, a, b]


def combine_vectors_kernel(last, bits, own_m, got_m, own_v, got_v, out):
    def body(left_m, left_v, right_m, right_v):
        a_left, c_right = vec(left_v, 0), vec(right_v, 1)
        a = plus(matvec(block(right_m, 0), a_left), vec(right_v, 0))
        middle = plus(matvec(block(right_m, 2), a_left), c_right)
        c = plus(matvec(block(left_m, 1), middle), vec(left_v, 1))
        for k in range(NVAR):
            out[0, k] = a[k]
            out[1, k] = c[k]

    @pl.when(bits[0, 0] == 0)
    def _():
        body(own_m, own_v, got_m, got_v)

    @pl.when(bits[0, 0] == 1)
    def _():
        body(got_m, got_v, own_m, own_v)


def combine_matrices_kernel(bits, own, got, out):
    def body(left, right):
        lines = left.shape[3]

        def group(g, _):
            here = pl.ds(pl.multiple_of(g * ROWS, ROWS), ROWS)

            def block_of(ref, which):
                return lambda a, b: ref[which, a, b, here]

            def whole(ref, which):
                return [ref[which, a, b, here] for a in range(NVAR) for b in range(NVAR)]

            def emit(which, matrix):
                for a in range(NVAR):
                    for b in range(NVAR):
                        out[which, a, b, here] = matrix[NVAR * a + b]

            a_left = whole(left, 0)
            emit(0, matmat(block_of(right, 0), a_left))
            through = matmat(block_of(right, 2), a_left)
            emit(2, plus(matmat(block_of(left, 1), through), whole(left, 2)))
            emit(1, matmat(block_of(left, 1), whole(right, 1)))
            return 0

        lax.fori_loop(0, lines // ROWS, group, 0)

    @pl.when(bits[0, 0] == 0)
    def _():
        body(own, got)

    @pl.when(bits[0, 0] == 1)
    def _():
        body(got, own)


def descend(levels, bits, refs, f_ref, b_ref):
    top = levels - 1
    own_m, got_c, own_v, got = refs[top]
    shape = f_ref.shape[1:]

    @pl.when(bits[top, 0] == 0)
    def _():
        b = plus(
            matvec(lambda a, b: got_c[a, b], vec(own_v, 0)),
            [got[k] for k in range(NVAR)],
        )
        for k in range(NVAR):
            f_ref[k] = jnp.zeros(shape, F32)
            b_ref[k] = b[k]

    @pl.when(bits[top, 0] == 1)
    def _():
        for k in range(NVAR):
            f_ref[k] = got[k]
            b_ref[k] = jnp.zeros(shape, F32)

    for l in reversed(range(top)):
        own_m, got_m, own_v, got_v = refs[l]

        @pl.when(bits[l, 0] == 0)
        def _(own_m=own_m, got_m=got_m, own_v=own_v, got_v=got_v):
            f = [f_ref[k] for k in range(NVAR)]
            b = [b_ref[k] for k in range(NVAR)]
            mid = plus(matvec(block(own_m, 0), f), vec(own_v, 0))
            out = plus(
                plus(matvec(block(got_m, 1), b), matvec(block(got_m, 2), mid)),
                vec(got_v, 1),
            )
            for k in range(NVAR):
                b_ref[k] = out[k]

        @pl.when(bits[l, 0] == 1)
        def _(own_m=own_m, got_m=got_m, own_v=own_v, got_v=got_v):
            f = [f_ref[k] for k in range(NVAR)]
            out = plus(matvec(block(got_m, 0), f), vec(got_v, 0))
            for k in range(NVAR):
                f_ref[k] = out[k]


def middle_kernel(
    levels, bits, *rest
):
    refs = [rest[4 * l : 4 * l + 4] for l in range(levels)]
    (source, x_lower, x_upper, y_inverse, y_lower, y_upper,
     reduced, y_source, f_ref, b_ref, held) = rest[4 * levels :]
    cells, rows = source.shape[1:3]
    descend(levels, bits, refs, f_ref, b_ref)

    def forward(i, v):
        product = matvec(lambda a, b: x_lower[a, b, i], list(v))
        v = [source[c, i] - product[c] for c in range(NVAR)]
        for c in range(NVAR):
            held[c, pl.ds(pl.multiple_of(i * rows, rows), rows)] = v[c]
        return tuple(v)

    lax.fori_loop(0, cells, forward, tuple(f_ref[k] for k in range(NVAR)))

    def backward(k, w):
        i = cells - 1 - k
        here = pl.ds(pl.multiple_of(i * rows, rows), rows)
        product = matvec(lambda a, b: x_upper[a, b, i], list(w))
        w = [held[c, here] - product[c] for c in range(NVAR)]
        s = matvec(lambda a, b: y_inverse[a, b, here], w)
        for c in range(NVAR):
            y_source[c, here] = s[c]
        return tuple(w)

    lax.fori_loop(0, cells, backward, tuple(b_ref[k] for k in range(NVAR)))

    def line(j):
        return pl.ds(j, cells, stride=rows)

    zero = jnp.zeros((cells, source.shape[3]), F32)

    def y_forward(j, v):
        product = matvec(lambda a, b: y_lower[a, b, line(j), :], list(v))
        v = [y_source[c, line(j), :] - product[c] for c in range(NVAR)]
        for c in range(NVAR):
            held[c, pl.ds(pl.multiple_of(j * cells, cells), cells)] = v[c]
        return tuple(v)

    v = lax.fori_loop(0, rows, y_forward, (zero,) * NVAR)

    def y_backward(k, w):
        j = rows - 1 - k
        product = matvec(lambda a, b: y_upper[a, b, line(j), :], list(w))
        here = pl.ds(pl.multiple_of(j * cells, cells), cells)
        return tuple(held[c, here] - product[c] for c in range(NVAR))

    w = lax.fori_loop(0, rows, y_backward, (zero,) * NVAR)
    for c in range(NVAR):
        reduced[0, c] = v[c]
        reduced[1, c] = w[c]


def end_kernel(levels, cells, rows, bits, *rest):
    refs = [rest[4 * l : 4 * l + 4] for l in range(levels)]
    y_source, y_lower, y_upper, out, f_ref, b_ref, held = rest[4 * levels :]
    descend(levels, bits, refs, f_ref, b_ref)

    def line(j):
        return pl.ds(j, cells, stride=rows)

    def forward(j, v):
        product = matvec(lambda a, b: y_lower[a, b, line(j), :], list(v))
        v = [y_source[c, line(j), :] - product[c] for c in range(NVAR)]
        for c in range(NVAR):
            held[c, pl.ds(pl.multiple_of(j * cells, cells), cells)] = v[c]
        return tuple(v)

    lax.fori_loop(0, rows, forward, tuple(f_ref[k] for k in range(NVAR)))

    def backward(k, w):
        j = rows - 1 - k
        here = pl.ds(pl.multiple_of(j * cells, cells), cells)
        product = matvec(lambda a, b: y_upper[a, b, line(j), :], list(w))
        w = [held[c, here] - product[c] for c in range(NVAR)]
        for c in range(NVAR):
            out[c, line(j), :] = w[c]
        return tuple(w)

    lax.fori_loop(0, rows, backward, tuple(b_ref[k] for k in range(NVAR)))


def per_device(field, forcing, x_inverse, x_lower, x_upper, y_inverse, y_lower, y_upper):
    cells, rows, lanes = field.shape[1:]
    n_px, n_py = lax.axis_size("px"), lax.axis_size("py")
    x_levels, y_levels = n_px.bit_length() - 1, n_py.bit_length() - 1

    def swap(value, axis, level):
        n = lax.axis_size(axis)
        return lax.ppermute(value, axis, [(i, i ^ (1 << level)) for i in range(n)])

    def shift(value, axis, step):
        n = lax.axis_size(axis)
        return lax.ppermute(
            value, axis, [(i, i + step) for i in range(n) if 0 <= i + step < n]
        )

    def bits_of(axis, levels):
        return ((lax.axis_index(axis) >> jnp.arange(levels)) & 1).astype(jnp.int32)[:, None]

    smem = pl.BlockSpec(memory_space=pltpu.SMEM)
    vmem = pl.BlockSpec(memory_space=pltpu.VMEM)

    def with_bits(kernel, name, out_shapes, operands, bits, scratch=()):
        shapes = [jax.ShapeDtypeStruct(s, F32) for s in out_shapes]
        single = len(shapes) == 1
        return pl.pallas_call(
            kernel,
            name=name,
            out_shape=shapes[0] if single else shapes,
            in_specs=[smem] + [vmem] * len(operands),
            out_specs=vmem if single else [vmem] * len(shapes),
            scratch_shapes=[pltpu.VMEM(s, F32) for s in scratch],
            compiler_params=pltpu.CompilerParams(vmem_limit_bytes=VMEM_BYTES),
        )(bits, *operands)

    x_bits, y_bits = bits_of("px", x_levels), bits_of("py", y_levels)

    y_before = shift(field[:, :, rows - 2 :], "py", 1)
    y_after = shift(field[:, :, :2], "py", -1)
    x_before = shift(field[:, cells - 2 :], "px", 1)
    x_after = shift(field[:, :2], "px", -1)

    flat = lambda m: m.reshape(m.shape[:2] + (cells * rows, lanes))
    y_inverse, y_lower, y_upper = flat(y_inverse), flat(y_lower), flat(y_upper)

    x_m = [call(compose_x_kernel, "compose_x", [(3, NVAR, NVAR, rows, lanes)],
                [(cells, NVAR * NVAR, ROWS, lanes)])(x_lower, x_upper)]
    y_m = [call(functools.partial(compose_y_kernel, cells, rows), "compose_y",
                [(3, NVAR, NVAR, cells, lanes)],
                [(rows, NVAR * NVAR, cells, lanes)])(y_lower, y_upper)]

    def exchange_matrices(own, axis, levels, bits):
        got = []
        for l in range(levels):
            if l == levels - 1:
                got.append(swap(own[l][2], axis, l))
            else:
                got.append(swap(own[l], axis, l))
                own.append(with_bits(combine_matrices_kernel, "join_matrices",
                                     [own[l].shape], [own[l], got[l]], bits[l:l + 1]))
        return got

    x_got_m = exchange_matrices(x_m, "px", x_levels, x_bits)
    y_got_m = exchange_matrices(y_m, "py", y_levels, y_bits)

    reduced, source = call(
        local_x_kernel, "local_x",
        [(2, NVAR, rows, lanes), (NVAR, cells, rows, lanes)],
        [(NVAR, cells + 4, rows + 2 * ROWS, lanes), (NVAR, cells, rows, lanes)],
    )(field, forcing, x_before, x_after, y_before, y_after, x_inverse, x_lower, x_upper)

    def exchange_vectors(own, axis, levels, bits, own_m, got_m):
        operands = []
        for l in range(levels):
            if l == levels - 1:
                send = jnp.where(bits[l, 0] == 0, own[0], own[1])
                got = swap(send, axis, l)
            else:
                got = swap(own, axis, l)
            operands += [own_m[l], got_m[l], own, got]
            if l < levels - 1:
                own = with_bits(functools.partial(combine_vectors_kernel, False), "join_vectors",
                                [own.shape], [own_m[l], got_m[l], own, got], bits[l:l + 1])
        return operands

    operands = exchange_vectors(reduced, "px", x_levels, x_bits, x_m, x_got_m)
    reduced, y_source = with_bits(
        functools.partial(middle_kernel, x_levels), "middle",
        [(2, NVAR, cells, lanes), (NVAR, cells * rows, lanes)],
        operands + [source, x_lower, x_upper, y_inverse, y_lower, y_upper],
        x_bits,
        [(NVAR, rows, lanes), (NVAR, rows, lanes), (NVAR, cells * rows, lanes)],
    )
    operands = exchange_vectors(reduced, "py", y_levels, y_bits, y_m, y_got_m)
    out = with_bits(
        functools.partial(end_kernel, y_levels, cells, rows), "end",
        [(NVAR, cells * rows, lanes)],
        operands + [y_source, y_lower, y_upper],
        y_bits,
        [(NVAR, cells, lanes), (NVAR, cells, lanes), (NVAR, cells * rows, lanes)],
    )
    return out.reshape(NVAR, cells, rows, lanes)


def solution(mesh):
    cell = P(None, "px", "py", None)
    blocks = P(None, None, "px", "py", None)
    return jax.shard_map(
        per_device,
        mesh=mesh,
        in_specs=(cell, cell) + (blocks,) * 6,
        out_specs=cell,
        check_vma=False,
    )
```

```python
import functools

import jax
import jax.numpy as jnp
from jax import lax
from jax.experimental import pallas as pl
from jax.experimental.pallas import tpu as pltpu
from jax.sharding import PartitionSpec as P

DISSIPATION = 0.1
NVAR = 5
F32 = jnp.float32
ROWS = 8
VMEM_BYTES = 12 * 1024 * 1024


def call(kernel, name, out_shapes, operands, scratch=(), result_in_hbm=False, from_hbm=(),
         copies=0):
    vmem = pl.BlockSpec(memory_space=pltpu.VMEM)
    make = jax.ShapeDtypeStruct if result_in_hbm else pltpu.VMEM
    shapes = [make(s, F32) for s in out_shapes]
    single = len(shapes) == 1
    operands = [pltpu.with_memory_space_constraint(x, pltpu.VMEM) for x in operands]
    outer = [pltpu.with_memory_space_constraint(x, pltpu.HBM) for x in from_hbm]
    semaphores = [pltpu.SemaphoreType.DMA((copies,))] if copies else []
    return pl.pallas_call(
        kernel,
        name=name,
        out_shape=shapes[0] if single else shapes,
        in_specs=[vmem] * len(operands) + [pl.BlockSpec(memory_space=pltpu.HBM)] * len(outer),
        out_specs=vmem if single else [vmem] * len(shapes),
        scratch_shapes=[pltpu.VMEM(s, F32) for s in scratch] + semaphores,
        compiler_params=pltpu.CompilerParams(vmem_limit_bytes=VMEM_BYTES),
    )(*operands, *outer)


class Loads:
    def __init__(self, semaphores):
        self.semaphores, self.used = semaphores, 0

    def start(self, source, target):
        copies = []
        for k in range(source.shape[0]):
            copy = pltpu.make_async_copy(source.at[k], target.at[k], self.semaphores.at[self.used])
            copy.start()
            copies.append(copy)
            self.used += 1
        return copies


def wait(copies):
    for copy in copies:
        copy.wait()


def hold(arrays, *others):
    def nothing(*refs):
        pass

    operands = [pltpu.with_memory_space_constraint(x, pltpu.VMEM) for x in (*arrays, *others)]
    anywhere = pl.BlockSpec(memory_space=pl.ANY)
    held = pl.pallas_call(
        nothing,
        name="hold",
        out_shape=[pltpu.VMEM(x.shape, F32) for x in arrays],
        in_specs=[anywhere] * len(operands),
        out_specs=[anywhere] * len(arrays),
        input_output_aliases={k: k for k in range(len(arrays))},
        compiler_params=pltpu.CompilerParams(vmem_limit_bytes=1024 * 1024),
    )(*operands)
    return list(held)


def bit(axis, level):
    return (lax.axis_index(axis) >> level) & 1


def tree(terms):
    while len(terms) > 1:
        pairs = [terms[k] + terms[k + 1] for k in range(0, len(terms) - 1, 2)]
        terms = pairs + (terms[-1:] if len(terms) % 2 else [])
    return terms[0]


def matvec(load, vector):
    return [tree([load(a, b) * vector[b] for b in range(NVAR)]) for a in range(NVAR)]


def matmat(load, matrix):
    out = []
    for a in range(NVAR):
        row = [load(a, b) for b in range(NVAR)]
        for c in range(NVAR):
            out.append(tree([row[b] * matrix[NVAR * b + c] for b in range(NVAR)]))
    return out


def plus(left, right):
    return [p + q for p, q in zip(left, right, strict=True)]


def minus(left, right):
    return [p - q for p, q in zip(left, right, strict=True)]


def compose_lines(length, lower_at, upper_at, store_p, load_p, emit, turn=lambda: None):
    first = [-lower_at(0, a, b) for a in range(NVAR) for b in range(NVAR)]
    store_p(0, first)

    def forward(i, p):
        p = [-q for q in matmat(lambda a, b: lower_at(i, a, b), p)]
        store_p(i, p)
        return tuple(p)

    last = lax.fori_loop(1, length, forward, tuple(first))
    emit(0, last)
    turn()

    def backward(k, carried):
        w, r = carried
        i = length - 1 - k
        here = [upper_at(i, a, b) for a in range(NVAR) for b in range(NVAR)]
        at = lambda a, b: here[NVAR * a + b]
        w = minus(load_p(i), matmat(at, list(w)))
        r = [-q for q in matmat(at, list(r))]
        return tuple(w), tuple(r)

    r = tuple(-upper_at(length - 1, a, b) for a in range(NVAR) for b in range(NVAR))
    w, r = lax.fori_loop(1, length, backward, (last, r))
    emit(1, r)
    emit(2, w)


def compose_x_kernel(lower, upper, forcing_hbm, x_inverse_hbm, y_inverse_hbm,
                     out, forcing, x_inverse, y_inverse, held, semaphores):
    loads = Loads(semaphores)
    copies = loads.start(forcing_hbm, forcing) + loads.start(x_inverse_hbm, x_inverse)
    copies += loads.start(y_inverse_hbm, y_inverse)
    cells, rows = lower.shape[2], lower.shape[3]

    def group(g, _):
        here = pl.ds(pl.multiple_of(g * ROWS, ROWS), ROWS)

        def emit(which, matrix):
            for a in range(NVAR):
                for b in range(NVAR):
                    out[which, a, b, here] = matrix[NVAR * a + b]

        def store_p(i, p):
            for k in range(NVAR * NVAR):
                held[i, k] = p[k]

        compose_lines(
            cells,
            lambda i, a, b: lower[a, b, i, here],
            lambda i, a, b: upper[a, b, i, here],
            store_p,
            lambda i: [held[i, k] for k in range(NVAR * NVAR)],
            emit,
        )
        return 0

    lax.fori_loop(0, rows // ROWS, group, 0)
    wait(copies)


def compose_y_kernel(cells_x, cells_y, lower_hbm, upper_hbm, x_lower_hbm, x_upper_hbm,
                     out, lower_t, upper_t, x_lower, x_upper, held, lower, upper, semaphores):
    loads = Loads(semaphores)
    first, second = loads.start(lower_hbm, lower), loads.start(upper_hbm, upper)
    others = loads.start(x_lower_hbm, x_lower) + loads.start(x_upper_hbm, x_upper)
    wait(first)

    def emit(which, matrix):
        for a in range(NVAR):
            for b in range(NVAR):
                out[which, a, b] = matrix[NVAR * a + b]

    def store_p(i, p):
        for k in range(NVAR * NVAR):
            held[i, k] = p[k]

    def at(ref, kept):
        def load(j, a, b):
            value = ref[a, b, pl.ds(j, cells_x, stride=cells_y), :]
            kept[j, NVAR * a + b] = value
            return value

        return load

    compose_lines(
        cells_y,
        at(lower, lower_t),
        at(upper, upper_t),
        store_p,
        lambda i: [held[i, k] for k in range(NVAR * NVAR)],
        emit,
        lambda: wait(second),
    )
    wait(others)


def local_x_kernel(
    field, forcing, x_pair, x_cross, y_pair, y_cross, inverse, lower, upper,
    reduced, source_out, padded, held,
):
    cells, rows, lanes = field.shape[1:]
    zero = jnp.zeros((rows, lanes), F32)
    middle = pl.ds(ROWS, rows)
    for c in range(NVAR):
        for i in range(cells):
            padded[c, i + 2, middle] = field[c, i]

    def y_before(value):
        for c in range(NVAR):
            for k in range(2):
                for i in range(cells):
                    padded[c, i + 2, ROWS - 2 + k] = value(c, k, i)

    def y_after(value):
        for c in range(NVAR):
            for k in range(2):
                for i in range(cells):
                    padded[c, i + 2, ROWS + rows + k] = value(c, k, i)

    def x_before(value):
        for c in range(NVAR):
            for k in range(2):
                padded[c, k, middle] = value(c, k)

    def x_after(value):
        for c in range(NVAR):
            for k in range(2):
                padded[c, cells + 2 + k, middle] = value(c, k)

    for axis, before, behind, pair, cross, empty in (
        ("px", x_before, x_after, x_pair, x_cross, jnp.zeros((rows, lanes), F32)),
        ("py", y_before, y_after, y_pair, y_cross, jnp.zeros((lanes,), F32)),
    ):
        at, count = lax.axis_index(axis), lax.axis_size(axis)

        @pl.when(bit(axis, 0) == 0)
        def _(before=before, behind=behind, pair=pair, cross=cross):
            before(lambda *k: cross[k])
            behind(lambda *k: pair[k])

        @pl.when(bit(axis, 0) == 1)
        def _(before=before, behind=behind, pair=pair, cross=cross):
            before(lambda *k: pair[k])
            behind(lambda *k: cross[k])

        @pl.when(at == 0)
        def _(before=before, empty=empty):
            before(lambda *k: empty)

        @pl.when(at == count - 1)
        def _(behind=behind, empty=empty):
            behind(lambda *k: empty)

    def right_side(i):
        out = []
        for c in range(NVAR):
            centre = padded[c, i + 2, middle]
            along_x = (
                padded[c, i, middle] - 4.0 * padded[c, i + 1, middle] + 6.0 * centre
                - 4.0 * padded[c, i + 3, middle] + padded[c, i + 4, middle]
            )
            along_y = (
                padded[c, i + 2, pl.ds(ROWS - 2, rows)]
                - 4.0 * padded[c, i + 2, pl.ds(ROWS - 1, rows)]
                + 6.0 * centre
                - 4.0 * padded[c, i + 2, pl.ds(ROWS + 1, rows)]
                + padded[c, i + 2, pl.ds(ROWS + 2, rows)]
            )
            out.append(forcing[c, i] - DISSIPATION * (along_x + along_y))
        return out

    def forward(i, v):
        s = matvec(lambda a, b: inverse[a, b, i], right_side(i))
        for c in range(NVAR):
            source_out[c, i] = s[c]
        v = minus(s, matvec(lambda a, b: lower[a, b, i], list(v)))
        for c in range(NVAR):
            held[c, i] = v[c]
        return tuple(v)

    v = lax.fori_loop(0, cells, forward, (zero,) * NVAR, unroll=True)
    for c in range(NVAR):
        reduced[0, c] = v[c]

    def backward(k, w):
        i = cells - 1 - k
        product = matvec(lambda a, b: upper[a, b, i], list(w))
        return tuple(held[c, i] - product[c] for c in range(NVAR))

    w = lax.fori_loop(0, cells, backward, (zero,) * NVAR, unroll=True)
    for c in range(NVAR):
        reduced[1, c] = w[c]


def vec(ref, which):
    return [ref[which, c] for c in range(NVAR)]


def block(ref, which):
    return lambda a, b: ref[which, a, b]


def pack_kernel(cells, rows, field, y_pair, y_cross, x_pair, x_cross):
    def y_layers(out, j):
        for c in range(NVAR):
            for k in range(2):
                out[c, k] = field[c, pl.ds(j + k, cells, stride=rows), :]

    def x_layers(out, i):
        for c in range(NVAR):
            for k in range(2):
                out[c, k] = field[c, pl.ds((i + k) * rows, rows), :]

    for axis, put, pair, cross, length in (
        ("py", y_layers, y_pair, y_cross, rows),
        ("px", x_layers, x_pair, x_cross, cells),
    ):

        @pl.when(bit(axis, 0) == 0)
        def _(put=put, pair=pair, cross=cross, length=length):
            put(pair, length - 2)
            put(cross, 0)

        @pl.when(bit(axis, 0) == 1)
        def _(put=put, pair=pair, cross=cross, length=length):
            put(pair, 0)
            put(cross, length - 2)


def join_vectors_kernel(axis, level, last, own_m, got_m, own_v, got_v, out):
    def union_a(left_v, right_m, right_v):
        return plus(matvec(block(right_m, 0), vec(left_v, 0)), vec(right_v, 0))

    def union_c(left_m, left_v, right_m, right_v):
        middle = plus(matvec(block(right_m, 2), vec(left_v, 0)), vec(right_v, 1))
        return plus(matvec(block(left_m, 1), middle), vec(left_v, 1))

    def body(left_m, left_v, right_m, right_v):
        if not last:
            a = union_a(left_v, right_m, right_v)
            c = union_c(left_m, left_v, right_m, right_v)
            for k in range(NVAR):
                out[0, k] = a[k]
                out[1, k] = c[k]
            return

        @pl.when(bit(axis, level + 1) == 0)
        def _():
            for k, value in enumerate(union_a(left_v, right_m, right_v)):
                out[k] = value

        @pl.when(bit(axis, level + 1) == 1)
        def _():
            for k, value in enumerate(union_c(left_m, left_v, right_m, right_v)):
                out[k] = value

    @pl.when(bit(axis, level) == 0)
    def _():
        body(own_m, own_v, got_m, got_v)

    @pl.when(bit(axis, level) == 1)
    def _():
        body(got_m, got_v, own_m, own_v)


def join_matrices_kernel(axis, level, last, own, got, out):
    def body(left, right):
        lines = left.shape[3]

        def group(g, _):
            here = pl.ds(pl.multiple_of(g * ROWS, ROWS), ROWS)

            def block_of(ref, which):
                return lambda a, b: ref[which, a, b, here]

            def whole(ref, which):
                return [ref[which, a, b, here] for a in range(NVAR) for b in range(NVAR)]

            def emit(which, matrix):
                for a in range(NVAR):
                    for b in range(NVAR):
                        if last:
                            out[a, b, here] = matrix[NVAR * a + b]
                        else:
                            out[which, a, b, here] = matrix[NVAR * a + b]

            a_left = whole(left, 0)
            through = matmat(block_of(right, 2), a_left)
            emit(2, plus(matmat(block_of(left, 1), through), whole(left, 2)))
            if not last:
                emit(0, matmat(block_of(right, 0), a_left))
                emit(1, matmat(block_of(left, 1), whole(right, 1)))
            return 0

        lax.fori_loop(0, lines // ROWS, group, 0)

    wanted = bit(axis, level + 1) == 1 if last else True

    @pl.when((bit(axis, level) == 0) & wanted)
    def _():
        body(own, got)

    @pl.when((bit(axis, level) == 1) & wanted)
    def _():
        body(got, own)


def descend(axis, levels, refs, f_ref, b_ref):
    top = levels - 1
    got_c, own, got = refs[4 * top : 4 * top + 3]
    shape = f_ref.shape[1:]

    @pl.when(bit(axis, top) == 0)
    def _():
        through = matvec(lambda a, b: got_c[a, b], [own[k] for k in range(NVAR)])
        for k in range(NVAR):
            f_ref[k] = jnp.zeros(shape, F32)
            b_ref[k] = through[k] + got[k]

    @pl.when(bit(axis, top) == 1)
    def _():
        for k in range(NVAR):
            f_ref[k] = got[k]
            b_ref[k] = jnp.zeros(shape, F32)

    for l in reversed(range(top)):
        own_m, got_m, own_v, got_v = refs[4 * l : 4 * l + 4]

        @pl.when(bit(axis, l) == 0)
        def _(own_m=own_m, got_m=got_m, own_v=own_v, got_v=got_v):
            f = [f_ref[k] for k in range(NVAR)]
            b = [b_ref[k] for k in range(NVAR)]
            mid = plus(matvec(block(own_m, 0), f), vec(own_v, 0))
            out = plus(
                plus(matvec(block(got_m, 1), b), matvec(block(got_m, 2), mid)),
                vec(got_v, 1),
            )
            for k in range(NVAR):
                b_ref[k] = out[k]

        @pl.when(bit(axis, l) == 1)
        def _(own_m=own_m, got_m=got_m, own_v=own_v, got_v=got_v):
            f = [f_ref[k] for k in range(NVAR)]
            out = plus(matvec(block(got_m, 0), f), vec(got_v, 0))
            for k in range(NVAR):
                f_ref[k] = out[k]


def middle_kernel(levels, *rest):
    (source, x_lower, x_upper, y_inverse, y_lower, y_upper,
     reduced, y_source, f_ref, b_ref, held) = rest[4 * levels - 1 :]
    cells, rows = source.shape[1:3]
    descend("px", levels, rest, f_ref, b_ref)

    def forward(i, v):
        product = matvec(lambda a, b: x_lower[a, b, i], list(v))
        v = [source[c, i] - product[c] for c in range(NVAR)]
        for c in range(NVAR):
            held[c, pl.ds(pl.multiple_of(i * rows, rows), rows)] = v[c]
        return tuple(v)

    lax.fori_loop(0, cells, forward, tuple(f_ref[k] for k in range(NVAR)), unroll=True)

    def backward(k, w):
        i = cells - 1 - k
        here = pl.ds(pl.multiple_of(i * rows, rows), rows)
        product = matvec(lambda a, b: x_upper[a, b, i], list(w))
        w = [held[c, here] - product[c] for c in range(NVAR)]
        s = matvec(lambda a, b: y_inverse[a, b, here], w)
        for c in range(NVAR):
            y_source[c, here] = s[c]
        return tuple(w)

    lax.fori_loop(0, cells, backward, tuple(b_ref[k] for k in range(NVAR)), unroll=True)

    def line(j):
        return pl.ds(j, cells, stride=rows)

    zero = jnp.zeros((cells, source.shape[3]), F32)

    def y_forward(j, v):
        product = matvec(lambda a, b: y_lower[j, NVAR * a + b], list(v))
        v = [y_source[c, line(j), :] - product[c] for c in range(NVAR)]
        for c in range(NVAR):
            held[c, pl.ds(pl.multiple_of(j * cells, cells), cells)] = v[c]
        return tuple(v)

    v = lax.fori_loop(0, rows, y_forward, (zero,) * NVAR, unroll=True)

    def y_backward(k, w):
        j = rows - 1 - k
        product = matvec(lambda a, b: y_upper[j, NVAR * a + b], list(w))
        here = pl.ds(pl.multiple_of(j * cells, cells), cells)
        return tuple(held[c, here] - product[c] for c in range(NVAR))

    w = lax.fori_loop(0, rows, y_backward, (zero,) * NVAR, unroll=True)
    for c in range(NVAR):
        reduced[0, c] = v[c]
        reduced[1, c] = w[c]


def end_kernel(levels, cells, rows, *rest):
    y_source, y_lower, y_upper, out, f_ref, b_ref, held = rest[4 * levels - 1 :]
    descend("py", levels, rest, f_ref, b_ref)

    def line(j):
        return pl.ds(j, cells, stride=rows)

    def forward(j, v):
        product = matvec(lambda a, b: y_lower[j, NVAR * a + b], list(v))
        v = [y_source[c, line(j), :] - product[c] for c in range(NVAR)]
        for c in range(NVAR):
            held[c, pl.ds(pl.multiple_of(j * cells, cells), cells)] = v[c]
        return tuple(v)

    lax.fori_loop(0, rows, forward, tuple(f_ref[k] for k in range(NVAR)), unroll=True)

    def backward(k, w):
        j = rows - 1 - k
        here = pl.ds(pl.multiple_of(j * cells, cells), cells)
        product = matvec(lambda a, b: y_upper[j, NVAR * a + b], list(w))
        w = [held[c, here] - product[c] for c in range(NVAR)]
        for c in range(NVAR):
            out[c, line(j), :] = w[c]
        return tuple(w)

    lax.fori_loop(0, rows, backward, tuple(b_ref[k] for k in range(NVAR)), unroll=True)


def per_device(field, forcing, x_inverse, x_lower, x_upper, y_inverse, y_lower, y_upper):
    cells, rows, lanes = field.shape[1:]
    x_levels = lax.axis_size("px").bit_length() - 1
    y_levels = lax.axis_size("py").bit_length() - 1

    def swap(value, axis, level):
        pairs = [(i, i ^ (1 << level)) for i in range(lax.axis_size(axis))]
        return lax.ppermute(value, axis, pairs)

    def across(value, axis):
        n = lax.axis_size(axis)
        pairs = [(i, (i + 1) % n) for i in range(1, n, 2)]
        return lax.ppermute(value, axis, pairs + [(j, i) for i, j in pairs])

    flat = lambda m: m.reshape(m.shape[:-3] + (cells * rows, lanes))
    y_inverse, y_lower, y_upper = flat(y_inverse), flat(y_lower), flat(y_upper)

    y_pair, y_cross, x_pair, x_cross = call(
        functools.partial(pack_kernel, cells, rows), "pack",
        [(NVAR, 2, cells, lanes)] * 2 + [(NVAR, 2, rows, lanes)] * 2,
        [flat(field)],
    )
    y_cross, x_cross = across(y_cross, "py"), across(x_cross, "px")
    y_pair, x_pair = swap(y_pair, "py", 0), swap(x_pair, "px", 0)
    halos = (x_pair, x_cross, y_pair, y_cross)

    def exchange(axis, levels, own_m, got_m, own_v, rest):
        operands = []
        for l in range(levels - 1):
            last = l == levels - 2
            next_m = call(functools.partial(join_matrices_kernel, axis, l, last),
                          "join_matrices", [own_m.shape[last:]], [own_m, got_m])
            next_got = swap(next_m, axis, l + 1)
            got_v = swap(own_v, axis, l)
            operands += [own_m, got_m, own_v, got_v]
            held = hold(operands + rest)
            operands, rest = held[: len(operands)], held[len(operands) :]
            own_v = call(functools.partial(join_vectors_kernel, axis, l, last),
                         "join_vectors", [own_v.shape[last:]], operands[-4:])
            own_m, got_m = next_m, next_got
            if not last:
                (got_m,) = hold([got_m], own_v)
        operands += [got_m, own_v, swap(own_v, axis, levels - 1)]
        held = hold(operands + rest)
        return held[: len(operands)], held[len(operands) :]

    y_m, y_lower, y_upper, x_lower, x_upper = call(
        functools.partial(compose_y_kernel, cells, rows), "compose_y",
        [(3, NVAR, NVAR, cells, lanes)] + [(rows, NVAR * NVAR, cells, lanes)] * 2
        + [x_lower.shape] * 2,
        [],
        [(rows, NVAR * NVAR, cells, lanes)] + [y_lower.shape] * 2,
        from_hbm=[y_lower, y_upper, x_lower, x_upper],
        copies=4 * NVAR,
    )
    x_m, forcing, x_inverse, y_inverse = call(
        compose_x_kernel, "compose_x",
        [(3, NVAR, NVAR, rows, lanes), forcing.shape, x_inverse.shape, y_inverse.shape],
        [x_lower, x_upper], [(cells, NVAR * NVAR, ROWS, lanes)],
        from_hbm=[forcing, x_inverse, y_inverse], copies=3 * NVAR,
    )
    kept = [y_m, x_m, forcing, x_inverse, y_inverse, x_lower, x_upper, y_lower, y_upper]
    kept = hold(kept, *halos)
    y_m, x_m, forcing, x_inverse, y_inverse, x_lower, x_upper, y_lower, y_upper = kept
    y_got, x_got = swap(y_m, "py", 0), swap(x_m, "px", 0)
    reduced, source = call(
        local_x_kernel, "local_x",
        [(2, NVAR, rows, lanes), (NVAR, cells, rows, lanes)],
        [field, forcing, *halos, x_inverse, x_lower, x_upper],
        [(NVAR, cells + 4, rows + 2 * ROWS, lanes), (NVAR, cells, rows, lanes)],
    )
    operands, rest = exchange(
        "px", x_levels, x_m, x_got, reduced,
        [source, x_lower, x_upper, y_inverse, y_lower, y_upper],
    )
    y_m, y_got = hold([y_m, y_got], operands[-1])
    reduced, source = call(
        functools.partial(middle_kernel, x_levels), "middle",
        [(2, NVAR, cells, lanes), (NVAR, cells * rows, lanes)],
        operands + rest,
        [(NVAR, rows, lanes), (NVAR, rows, lanes), (NVAR, cells * rows, lanes)],
    )
    operands, rest = exchange("py", y_levels, y_m, y_got, reduced, [source, *rest[-2:]])
    out = call(
        functools.partial(end_kernel, y_levels, cells, rows), "end",
        [(NVAR, cells * rows, lanes)],
        operands + rest,
        [(NVAR, cells, lanes), (NVAR, cells, lanes), (NVAR, cells * rows, lanes)],
        result_in_hbm=True,
    )
    return out.reshape(NVAR, cells, rows, lanes)


def solution(mesh):
    cell = P(None, "px", "py", None)
    blocks = P(None, None, "px", "py", None)
    return jax.shard_map(
        per_device,
        mesh=mesh,
        in_specs=(cell, cell) + (blocks,) * 6,
        out_specs=cell,
        check_vma=False,
    )
```

```python
import functools

import jax
import jax.numpy as jnp
from jax import lax
from jax.experimental import pallas as pl
from jax.experimental.pallas import tpu as pltpu
from jax.sharding import PartitionSpec as P

DISSIPATION = 0.1
NVAR = 5
F32 = jnp.float32
ROWS = 8
UNROLL = 3
MATRICES = 3 * NVAR * NVAR
VX = 5
PIECES = {"px": (25,), "py": (13, 12)}
VMEM_BYTES = 12 * 1024 * 1024


def call(kernel, name, out_shapes, operands, scratch=(), result_in_hbm=False, from_hbm=(),
         copies=0):
    vmem = pl.BlockSpec(memory_space=pltpu.VMEM)
    make = jax.ShapeDtypeStruct if result_in_hbm else pltpu.VMEM
    shapes = [make(s, F32) for s in out_shapes]
    single = len(shapes) == 1
    operands = [pltpu.with_memory_space_constraint(x, pltpu.VMEM) for x in operands]
    outer = [pltpu.with_memory_space_constraint(x, pltpu.HBM) for x in from_hbm]
    semaphores = [pltpu.SemaphoreType.DMA((copies,))] if copies else []
    return pl.pallas_call(
        kernel,
        name=name,
        out_shape=shapes[0] if single else shapes,
        in_specs=[vmem] * len(operands) + [pl.BlockSpec(memory_space=pltpu.HBM)] * len(outer),
        out_specs=vmem if single else [vmem] * len(shapes),
        scratch_shapes=[pltpu.VMEM(s, F32) for s in scratch] + semaphores,
        compiler_params=pltpu.CompilerParams(vmem_limit_bytes=VMEM_BYTES),
    )(*operands, *outer)


def hold(arrays, *others):
    def nothing(*refs):
        pass

    operands = [pltpu.with_memory_space_constraint(x, pltpu.VMEM) for x in (*arrays, *others)]
    anywhere = pl.BlockSpec(memory_space=pl.ANY)
    held = pl.pallas_call(
        nothing,
        name="hold",
        out_shape=[pltpu.VMEM(x.shape, F32) for x in arrays],
        in_specs=[anywhere] * len(operands),
        out_specs=[anywhere] * len(arrays),
        input_output_aliases={k: k for k in range(len(arrays))},
        compiler_params=pltpu.CompilerParams(vmem_limit_bytes=1024 * 1024),
    )(*operands)
    return list(held)


def bit(axis, level):
    return (lax.axis_index(axis) >> level) & 1


def tree(terms):
    while len(terms) > 1:
        pairs = [terms[k] + terms[k + 1] for k in range(0, len(terms) - 1, 2)]
        terms = pairs + (terms[-1:] if len(terms) % 2 else [])
    return terms[0]


def matvec(load, vector):
    return [tree([load(a, b) * vector[b] for b in range(NVAR)]) for a in range(NVAR)]


def matmat(load, matrix):
    out = []
    for a in range(NVAR):
        row = [load(a, b) for b in range(NVAR)]
        for c in range(NVAR):
            out.append(tree([row[b] * matrix[NVAR * b + c] for b in range(NVAR)]))
    return out


def plus(left, right):
    return [p + q for p, q in zip(left, right, strict=True)]


def minus(left, right):
    return [p - q for p, q in zip(left, right, strict=True)]


def compose_lines(length, lower_at, upper_at, store_p, load_p, emit):
    entries = [(a, b) for a in range(NVAR) for b in range(NVAR)]
    signed = lambda m: [-q for q in m] if length % 2 else list(m)
    first = [lower_at(0, a, b) for a, b in entries]
    store_p(0, first)

    def forward(i, p):
        p = matmat(lambda a, b: lower_at(i, a, b), p)
        store_p(i, p)
        return tuple(p)

    last = lax.fori_loop(1, length, forward, tuple(first), unroll=UNROLL)
    emit(0, signed(last))

    def backward(k, carried):
        w, r = carried
        i = length - 1 - k
        here = [upper_at(i, a, b) for a, b in entries]
        at = lambda a, b: here[NVAR * a + b]
        return tuple(plus(load_p(i), matmat(at, w))), tuple(matmat(at, r))

    r = tuple(upper_at(length - 1, a, b) for a, b in entries)
    w, r = lax.fori_loop(1, length, backward, (last, r), unroll=UNROLL)
    emit(1, signed(r))
    emit(2, [-q for q in w])


def compose_x_kernel(cells, lower, upper, _, field, y_inverse_hbm, out, y_inverse, held, semaphores):
    load = pltpu.make_async_copy(y_inverse_hbm, y_inverse, semaphores.at[0])
    load.start()
    rows = lower.shape[3]

    for side, first in enumerate((cells - 2, 0)):

        @pl.when(bit("px", 0) == side)
        def _(first=first):
            for c in range(NVAR):
                for k in range(2):
                    out[MATRICES + 2 * c + k] = field[c, pl.ds((first + k) * rows, rows), :]

    def group(g, _):
        here = pl.ds(pl.multiple_of(g * ROWS, ROWS), ROWS)

        def emit(which, matrix):
            for a in range(NVAR):
                for b in range(NVAR):
                    out[entry(which, a, b), here] = matrix[NVAR * a + b]

        def store_p(i, p):
            for k in range(NVAR * NVAR):
                held[i, k] = p[k]

        compose_lines(
            cells,
            lambda i, a, b: lower[a, b, i, here],
            lambda i, a, b: upper[a, b, i, here],
            store_p,
            lambda i: [held[i, k] for k in range(NVAR * NVAR)],
            emit,
        )
        return 0

    lax.fori_loop(0, rows // ROWS, group, 0)
    load.wait()


def compose_y_kernel(lower, upper, out, held):
    cells_y = lower.shape[1]

    def emit(which, matrix):
        for a in range(NVAR):
            for b in range(NVAR):
                out[entry(which, a, b)] = matrix[NVAR * a + b]

    def store_p(i, p):
        for k in range(NVAR * NVAR):
            held[i, k] = p[k]

    compose_lines(
        cells_y,
        lambda j, a, b: lower[NVAR * a + b, j],
        lambda j, a, b: upper[NVAR * a + b, j],
        store_p,
        lambda i: [held[i, k] for k in range(NVAR * NVAR)],
        emit,
    )


def local_x_kernel(
    field, forcing, x_got, x_cross, y_pair, y_cross, inverse, lower, upper,
    reduced, source_out, padded, held,
):
    cells, rows, lanes = field.shape[1:]
    zero = jnp.zeros((rows, lanes), F32)
    middle = pl.ds(ROWS, rows)
    for c in range(NVAR):
        for i in range(cells):
            padded[c, i + 2, middle] = field[c, i]

    def x_pair(c, k):
        return x_got[MATRICES + 2 * c + k]

    def y_before(value):
        for c in range(NVAR):
            for k in range(2):
                for i in range(cells):
                    padded[c, i + 2, ROWS - 2 + k] = value(c, k, i)

    def y_after(value):
        for c in range(NVAR):
            for k in range(2):
                for i in range(cells):
                    padded[c, i + 2, ROWS + rows + k] = value(c, k, i)

    def x_before(value):
        for c in range(NVAR):
            for k in range(2):
                padded[c, k, middle] = value(c, k)

    def x_after(value):
        for c in range(NVAR):
            for k in range(2):
                padded[c, cells + 2 + k, middle] = value(c, k)

    for axis, before, behind, pair, cross, empty in (
        ("px", x_before, x_after, x_pair, x_cross, jnp.zeros((rows, lanes), F32)),
        ("py", y_before, y_after, lambda *k: y_pair[k], y_cross, jnp.zeros((lanes,), F32)),
    ):
        at, count = lax.axis_index(axis), lax.axis_size(axis)

        @pl.when(bit(axis, 0) == 0)
        def _(before=before, behind=behind, pair=pair, cross=cross):
            before(lambda *k: cross[k])
            behind(pair)

        @pl.when(bit(axis, 0) == 1)
        def _(before=before, behind=behind, pair=pair, cross=cross):
            before(pair)
            behind(lambda *k: cross[k])

        @pl.when(at == 0)
        def _(before=before, empty=empty):
            before(lambda *k: empty)

        @pl.when(at == count - 1)
        def _(behind=behind, empty=empty):
            behind(lambda *k: empty)

    def right_side(i):
        out = []
        for c in range(NVAR):
            centre = padded[c, i + 2, middle]
            along_x = (
                padded[c, i, middle] - 4.0 * padded[c, i + 1, middle] + 6.0 * centre
                - 4.0 * padded[c, i + 3, middle] + padded[c, i + 4, middle]
            )
            along_y = (
                padded[c, i + 2, pl.ds(ROWS - 2, rows)]
                - 4.0 * padded[c, i + 2, pl.ds(ROWS - 1, rows)]
                + 6.0 * centre
                - 4.0 * padded[c, i + 2, pl.ds(ROWS + 1, rows)]
                + padded[c, i + 2, pl.ds(ROWS + 2, rows)]
            )
            out.append(forcing[c, i] - DISSIPATION * (along_x + along_y))
        return out

    def forward(i, v):
        s = matvec(lambda a, b: inverse[a, b, i], right_side(i))
        for c in range(NVAR):
            source_out[c, i] = s[c]
        v = minus(s, matvec(lambda a, b: lower[a, b, i], list(v)))
        for c in range(NVAR):
            held[c, i] = v[c]
        return tuple(v)

    v = lax.fori_loop(0, cells, forward, (zero,) * NVAR, unroll=True)
    for c in range(NVAR):
        reduced[0, c] = v[c]

    def backward(k, w):
        i = cells - 1 - k
        product = matvec(lambda a, b: upper[a, b, i], list(w))
        return tuple(held[c, i] - product[c] for c in range(NVAR))

    w = lax.fori_loop(0, cells, backward, (zero,) * NVAR, unroll=True)
    for c in range(NVAR):
        reduced[1, c] = w[c]


def vec(ref, which):
    return [ref[which, c] for c in range(NVAR)]


def entry(which, a, b):
    return (which * NVAR + a) * NVAR + b


def block(matrices, which, rows=slice(None)):
    return lambda a, b: matrices[entry(which, a, b), rows]


def whole(load):
    return [load(a, b) for a in range(NVAR) for b in range(NVAR)]


def in_order(axis, level, radix, bundles, then):
    place = (lax.axis_index(axis) >> level) & (radix - 1)
    for q in range(radix):

        @pl.when(place == q)
        def _(q=q):
            then(q, [bundles[m ^ q] for m in range(radix)])


def pack_kernel(cells, rows, field_hbm, lower_hbm, upper_hbm,
                y_pair, y_cross, x_cross, field, lower, upper, semaphores):
    first = pltpu.make_async_copy(field_hbm, field, semaphores.at[0])
    first.start()
    copies = []
    for source, target in ((lower_hbm, lower), (upper_hbm, upper)):
        for x in range(cells):
            copy = pltpu.make_async_copy(
                source.at[:, pl.ds(x * rows, rows), :],
                target.at[:, :, x, :],
                semaphores.at[1 + len(copies)],
            )
            copy.start()
            copies.append(copy)
    first.wait()

    def y_layers(out, j):
        for c in range(NVAR):
            for k in range(2):
                out[c, k] = field[c, pl.ds(j + k, cells, stride=rows), :]

    def x_layers(out, i):
        for c in range(NVAR):
            for k in range(2):
                out[c, k] = field[c, pl.ds((i + k) * rows, rows), :]

    @pl.when(bit("py", 0) == 0)
    def _():
        y_layers(y_pair, rows - 2)
        y_layers(y_cross, 0)

    @pl.when(bit("py", 0) == 1)
    def _():
        y_layers(y_pair, 0)
        y_layers(y_cross, rows - 2)

    for side, first_layer in enumerate((0, cells - 2)):

        @pl.when(bit("px", 0) == side)
        def _(first_layer=first_layer):
            x_layers(x_cross, first_layer)

    for copy in copies:
        copy.wait()


def grouped(refs, radix):
    return list(zip(refs[:radix], refs[radix : 2 * radix], strict=True))


def inflows(group, f):
    out = [f]
    for matrices, vectors in group:
        a = vec(vectors, 0)
        f = a if f is None else plus(matvec(block(matrices, 0), f), a)
        out.append(f)
    return out


def outflow(stretch, f, b):
    matrices, vectors = stretch
    out = vec(vectors, 1)
    if f is not None:
        out = plus(out, matvec(block(matrices, 2), f))
    if b is not None:
        out = plus(out, matvec(block(matrices, 1), b))
    return out


def join_vectors_kernel(axis, level, radix, last, *refs):
    out = refs[-1]

    def union_a(group):
        return inflows(group, None)[-1]

    def union_c(group):
        f, b = inflows(group[:-1], None), None
        for k in reversed(range(radix)):
            b = outflow(group[k], f[k], b)
        return b

    def then(q, group):
        if not last:
            for which, values in enumerate((union_a(group), union_c(group))):
                for k in range(NVAR):
                    out[which, k] = values[k]
            return

        for side, union in enumerate((union_a, union_c)):

            @pl.when(bit(axis, level + radix.bit_length() - 1) == side)
            def _(union=union):
                for k, value in enumerate(union(group)):
                    out[k] = value

    in_order(axis, level, radix, grouped(refs, radix), then)


def piece_of(axis, k):
    for piece, size in enumerate(PIECES[axis]):
        if k < size:
            return piece, k
        k -= size


def join_matrices_kernel(axis, level, radix, last, *refs):
    bundles, outs = refs[:radix], refs[radix:]
    lines = outs[0].shape[-2]

    def then(q, group):
        def register(g, _):
            here = pl.ds(pl.multiple_of(g * ROWS, ROWS), ROWS)
            at = lambda m, which: block(m, which, here)

            def emit(which, matrix):
                for k, value in enumerate(matrix):
                    if last:
                        piece, at_k = piece_of(axis, k)
                        outs[piece][at_k, here] = value
                    else:
                        outs[0][which * NVAR * NVAR + k, here] = value

            f = [None, whole(at(group[0], 0))]
            for m in group[1:-1]:
                f.append(matmat(at(m, 0), f[-1]))
            if not last:
                emit(0, matmat(at(group[-1], 0), f[-1]))
                r = whole(at(group[-1], 1))
                for m in reversed(group[:-1]):
                    r = matmat(at(m, 1), r)
                emit(1, r)
            c = matmat(at(group[-1], 2), f[-1])
            for k in reversed(range(1, radix - 1)):
                c = plus(matmat(at(group[k], 1), c), matmat(at(group[k], 2), f[k]))
            emit(2, plus(matmat(at(group[0], 1), c), whole(at(group[0], 2))))
            return 0

        lax.fori_loop(0, lines // ROWS, register, 0)

    wanted = bit(axis, level + radix.bit_length() - 1) == 1 if last else True

    @pl.when(wanted)
    def _():
        in_order(axis, level, radix, bundles, then)


def descend(axis, radices, refs, f_ref, b_ref):
    sizes = [2 * r for r in radices[:-1]]
    levels = [sum(r.bit_length() - 1 for r in radices[:t]) for t in range(len(radices))]
    *c_pieces, own, got = refs[sum(sizes) : descend_count(axis, radices)]
    shape = f_ref.shape[1:]

    def got_c(a, b):
        piece, at_k = piece_of(axis, NVAR * a + b)
        return c_pieces[piece][at_k]

    @pl.when(bit(axis, levels[-1]) == 0)
    def _():
        through = matvec(got_c, [own[k] for k in range(NVAR)])
        for k in range(NVAR):
            f_ref[k] = jnp.zeros(shape, F32)
            b_ref[k] = through[k] + got[k]

    @pl.when(bit(axis, levels[-1]) == 1)
    def _():
        for k in range(NVAR):
            f_ref[k] = got[k]
            b_ref[k] = jnp.zeros(shape, F32)

    for t in reversed(range(len(radices) - 1)):
        radix, first = radices[t], sum(sizes[:t])

        def then(q, group, radix=radix):
            f = inflows(group[:-1], [f_ref[k] for k in range(NVAR)])
            b = [b_ref[k] for k in range(NVAR)]
            for k in reversed(range(q + 1, radix)):
                b = outflow(group[k], f[k], b)
            for k in range(NVAR):
                f_ref[k] = f[q][k]
                b_ref[k] = b[k]

        here = grouped(refs[first : first + sizes[t]], radix)
        in_order(axis, levels[t], radix, here, then)


def descend_count(axis, radices):
    return sum(2 * r for r in radices[:-1]) + len(PIECES[axis]) + 2


def middle_kernel(radices, *rest):
    (source, x_lower, x_upper, y_inverse, y_lower, y_upper,
     reduced, y_source, f_ref, b_ref, held) = rest[descend_count("px", radices) :]
    cells, rows = source.shape[1:3]
    descend("px", radices, rest, f_ref, b_ref)

    def forward(i, v):
        product = matvec(lambda a, b: x_lower[a, b, i], list(v))
        v = [source[c, i] - product[c] for c in range(NVAR)]
        for c in range(NVAR):
            held[c, pl.ds(pl.multiple_of(i * rows, rows), rows)] = v[c]
        return tuple(v)

    lax.fori_loop(0, cells, forward, tuple(f_ref[k] for k in range(NVAR)), unroll=True)

    def backward(k, w):
        i = cells - 1 - k
        here = pl.ds(pl.multiple_of(i * rows, rows), rows)
        product = matvec(lambda a, b: x_upper[a, b, i], list(w))
        w = [held[c, here] - product[c] for c in range(NVAR)]
        s = matvec(lambda a, b: y_inverse[a, b, here], w)
        for c in range(NVAR):
            y_source[c, here] = s[c]
        return tuple(w)

    lax.fori_loop(0, cells, backward, tuple(b_ref[k] for k in range(NVAR)), unroll=True)

    def line(j):
        return pl.ds(j, cells, stride=rows)

    zero = jnp.zeros((cells, source.shape[3]), F32)

    def y_forward(j, v):
        product = matvec(lambda a, b: y_lower[NVAR * a + b, j], list(v))
        v = [y_source[c, line(j), :] - product[c] for c in range(NVAR)]
        for c in range(NVAR):
            held[c, pl.ds(pl.multiple_of(j * cells, cells), cells)] = v[c]
        return tuple(v)

    v = lax.fori_loop(0, rows, y_forward, (zero,) * NVAR, unroll=True)

    def y_backward(k, w):
        j = rows - 1 - k
        product = matvec(lambda a, b: y_upper[NVAR * a + b, j], list(w))
        here = pl.ds(pl.multiple_of(j * cells, cells), cells)
        return tuple(held[c, here] - product[c] for c in range(NVAR))

    w = lax.fori_loop(0, rows, y_backward, (zero,) * NVAR, unroll=True)
    for c in range(NVAR):
        reduced[0, c] = v[c]
        reduced[1, c] = w[c]


def end_kernel(radices, cells, rows, *rest):
    first = descend_count("py", radices)
    y_source, y_lower, y_upper, out, f_ref, b_ref, held = rest[first:]
    descend("py", radices, rest, f_ref, b_ref)

    def line(j):
        return pl.ds(j, cells, stride=rows)

    def forward(j, v):
        product = matvec(lambda a, b: y_lower[NVAR * a + b, j], list(v))
        v = [y_source[c, line(j), :] - product[c] for c in range(NVAR)]
        for c in range(NVAR):
            held[c, pl.ds(pl.multiple_of(j * cells, cells), cells)] = v[c]
        return tuple(v)

    lax.fori_loop(0, rows, forward, tuple(f_ref[k] for k in range(NVAR)), unroll=True)

    def backward(k, w):
        j = rows - 1 - k
        here = pl.ds(pl.multiple_of(j * cells, cells), cells)
        product = matvec(lambda a, b: y_upper[NVAR * a + b, j], list(w))
        w = [held[c, here] - product[c] for c in range(NVAR)]
        for c in range(NVAR):
            out[c, line(j), :] = w[c]
        return tuple(w)

    lax.fori_loop(0, rows, backward, tuple(b_ref[k] for k in range(NVAR)), unroll=True)


def radices_of(count):
    out, rest = [], count // 2
    while rest > 1:
        out.append(4 if rest % 4 == 0 else 2)
        rest //= out[-1]
    return out + [2]


def per_device(field, forcing, x_inverse, x_lower, x_upper, y_inverse, y_lower, y_upper):
    cells, rows, lanes = field.shape[1:]
    x_radices, y_radices = radices_of(lax.axis_size("px")), radices_of(lax.axis_size("py"))

    def swap(value, axis, step):
        pairs = [(i, i ^ step) for i in range(lax.axis_size(axis))]
        return lax.ppermute(value, axis, pairs)

    def across(value, axis):
        n = lax.axis_size(axis)
        pairs = [(i, (i + 1) % n) for i in range(1, n, 2)]
        return lax.ppermute(value, axis, pairs + [(j, i) for i, j in pairs])

    flat = lambda m: m.reshape(m.shape[:-3] + (cells * rows, lanes))
    y_inverse = flat(y_inverse)

    every = NVAR * NVAR
    y_pair, y_cross, x_cross, field, y_lower, y_upper = call(
        functools.partial(pack_kernel, cells, rows), "pack",
        [(NVAR, 2, cells, lanes)] * 2 + [(NVAR, 2, rows, lanes)]
        + [(NVAR, cells * rows, lanes)] + [(every, rows, cells, lanes)] * 2,
        [],
        from_hbm=[flat(field)] + [m.reshape(every, cells * rows, lanes) for m in (y_lower, y_upper)],
        copies=1 + 2 * cells,
    )
    field = field.reshape(NVAR, cells, rows, lanes)
    y_cross, x_cross = across(y_cross, "py"), across(x_cross, "px")
    y_pair = swap(y_pair, "py", 1)
    halos = (x_cross, y_pair, y_cross)

    def exchange(axis, radices, own_m, got_m, own_v, rest):
        operands, level = [], 0
        for t, radix in enumerate(radices[:-1]):
            last = t == len(radices) - 2
            settings = (axis, level, radix, last)
            got_v = [swap(own_v, axis, k << level) for k in range(1, radix)]
            lines = own_m.shape[1:]
            sizes = PIECES[axis] if last else (MATRICES,)
            next_m = call(functools.partial(join_matrices_kernel, *settings), "join_matrices",
                          [(size, *lines) for size in sizes], [own_m, *got_m])
            next_m = list(next_m) if len(sizes) > 1 else [next_m]
            next_level = level + radix.bit_length() - 1
            next_got = [swap(m, axis, k << next_level)
                        for k in range(1, radices[t + 1]) for m in next_m]
            count = len(operands)
            operands += [own_m, *got_m, own_v, *got_v]
            held = hold(operands + rest)
            operands, rest = held[: len(operands)], held[len(operands) :]
            own_v = call(functools.partial(join_vectors_kernel, *settings), "join_vectors",
                         [own_v.shape[last:]], operands[count:])
            if not last:
                next_got = hold(next_got, own_v)
            own_m, got_m, level = next_m[0], next_got, next_level
        operands += [*got_m, own_v, swap(own_v, axis, 1 << level)]
        held = hold(operands + rest)
        return held[: len(operands)], held[len(operands) :]

    y_m = call(compose_y_kernel, "compose_y", [(MATRICES, cells, lanes)],
               [y_lower, y_upper], [(rows, every, cells, lanes)])
    x_m, y_inverse = call(
        functools.partial(compose_x_kernel, cells), "compose_x",
        [(MATRICES + 2 * NVAR, rows, lanes), y_inverse.shape],
        [x_lower, x_upper, y_m, flat(field)], [(cells, every, ROWS, lanes)],
        from_hbm=[y_inverse], copies=1,
    )
    y_m, y_lower, y_upper, y_inverse, x_m = hold([y_m, y_lower, y_upper, y_inverse, x_m], *halos)
    y_got = [swap(y_m, "py", k) for k in range(1, y_radices[0])]
    x_got = [swap(x_m, "px", k) for k in range(1, x_radices[0])]
    reduced, source = call(
        local_x_kernel, "local_x",
        [(VX, NVAR, rows, lanes), (NVAR, cells, rows, lanes)],
        [field, forcing, x_got[0], *halos, x_inverse, x_lower, x_upper],
        [(NVAR, cells + 4, rows + 2 * ROWS, lanes), (NVAR, cells, rows, lanes)],
    )
    operands, (source, y_inverse, y_lower, y_upper) = exchange(
        "px", x_radices, x_m, x_got, reduced, [source, y_inverse, y_lower, y_upper]
    )
    reduced, source = call(
        functools.partial(middle_kernel, x_radices), "middle",
        [(2, NVAR, cells, lanes), (NVAR, cells * rows, lanes)],
        [*operands, source, x_lower, x_upper, y_inverse, y_lower, y_upper],
        [(NVAR, rows, lanes), (NVAR, rows, lanes), (NVAR, cells * rows, lanes)],
    )
    y_m, *y_got = hold([y_m, *y_got], reduced)
    operands, rest = exchange(
        "py", y_radices, y_m, y_got, reduced, [source, y_lower, y_upper]
    )
    out = call(
        functools.partial(end_kernel, y_radices, cells, rows), "end",
        [(NVAR, cells * rows, lanes)],
        operands + rest,
        [(NVAR, cells, lanes), (NVAR, cells, lanes), (NVAR, cells * rows, lanes)],
        result_in_hbm=True,
    )
    return out.reshape(NVAR, cells, rows, lanes)


def solution(mesh):
    cell = P(None, "px", "py", None)
    blocks = P(None, None, "px", "py", None)
    return jax.shard_map(
        per_device,
        mesh=mesh,
        in_specs=(cell, cell) + (blocks,) * 6,
        out_specs=cell,
        check_vma=False,
    )
```

```python
import functools

import jax
import jax.numpy as jnp
from jax import lax
from jax.experimental import pallas as pl
from jax.experimental.pallas import tpu as pltpu
from jax.sharding import PartitionSpec as P

DISSIPATION = 0.1
NVAR = 5
F32 = jnp.float32
ROWS = 8
UNROLL = 3
MATRICES = 3 * NVAR * NVAR
VX = 2
PIECES = {"px": (25,), "py": (13, 12)}
VMEM_BYTES = 12 * 1024 * 1024


def call(kernel, name, out_shapes, operands, scratch=(), result_in_hbm=False, from_hbm=(),
         copies=0):
    vmem = pl.BlockSpec(memory_space=pltpu.VMEM)
    make = jax.ShapeDtypeStruct if result_in_hbm else pltpu.VMEM
    shapes = [make(s, F32) for s in out_shapes]
    single = len(shapes) == 1
    operands = [pltpu.with_memory_space_constraint(x, pltpu.VMEM) for x in operands]
    outer = [pltpu.with_memory_space_constraint(x, pltpu.HBM) for x in from_hbm]
    semaphores = [pltpu.SemaphoreType.DMA((copies,))] if copies else []
    return pl.pallas_call(
        kernel,
        name=name,
        out_shape=shapes[0] if single else shapes,
        in_specs=[vmem] * len(operands) + [pl.BlockSpec(memory_space=pltpu.HBM)] * len(outer),
        out_specs=vmem if single else [vmem] * len(shapes),
        scratch_shapes=[pltpu.VMEM(s, F32) for s in scratch] + semaphores,
        compiler_params=pltpu.CompilerParams(vmem_limit_bytes=VMEM_BYTES),
    )(*operands, *outer)


def hold(arrays, *others):
    def nothing(*refs):
        pass

    operands = [pltpu.with_memory_space_constraint(x, pltpu.VMEM) for x in (*arrays, *others)]
    anywhere = pl.BlockSpec(memory_space=pl.ANY)
    held = pl.pallas_call(
        nothing,
        name="hold",
        out_shape=[pltpu.VMEM(x.shape, F32) for x in arrays],
        in_specs=[anywhere] * len(operands),
        out_specs=[anywhere] * len(arrays),
        input_output_aliases={k: k for k in range(len(arrays))},
        compiler_params=pltpu.CompilerParams(vmem_limit_bytes=1024 * 1024),
    )(*operands)
    return list(held)


def bit(axis, level):
    return (lax.axis_index(axis) >> level) & 1


def tree(terms):
    while len(terms) > 1:
        pairs = [terms[k] + terms[k + 1] for k in range(0, len(terms) - 1, 2)]
        terms = pairs + (terms[-1:] if len(terms) % 2 else [])
    return terms[0]


def matvec(load, vector):
    return [tree([load(a, b) * vector[b] for b in range(NVAR)]) for a in range(NVAR)]


def matmat(load, matrix):
    out = []
    for a in range(NVAR):
        row = [load(a, b) for b in range(NVAR)]
        for c in range(NVAR):
            out.append(tree([row[b] * matrix[NVAR * b + c] for b in range(NVAR)]))
    return out


def plus(left, right):
    return [p + q for p, q in zip(left, right, strict=True)]


def minus(left, right):
    return [p - q for p, q in zip(left, right, strict=True)]


def compose_lines(length, lower_at, upper_at, store_p, load_p, emit):
    entries = [(a, b) for a in range(NVAR) for b in range(NVAR)]
    signed = lambda m: [-q for q in m] if length % 2 else list(m)
    first = [lower_at(0, a, b) for a, b in entries]
    store_p(0, first)

    def forward(i, p):
        p = matmat(lambda a, b: lower_at(i, a, b), p)
        store_p(i, p)
        return tuple(p)

    last = lax.fori_loop(1, length, forward, tuple(first), unroll=UNROLL)
    emit(0, signed(last))

    def backward(k, carried):
        w, r = carried
        i = length - 1 - k
        here = [upper_at(i, a, b) for a, b in entries]
        at = lambda a, b: here[NVAR * a + b]
        return tuple(plus(load_p(i), matmat(at, w))), tuple(matmat(at, r))

    r = tuple(upper_at(length - 1, a, b) for a, b in entries)
    w, r = lax.fori_loop(1, length, backward, (last, r), unroll=UNROLL)
    emit(1, signed(r))
    emit(2, [-q for q in w])


def compose_x(lower, upper, out, held):
    cells, rows = lower.shape[2:4]

    def group(g, _):
        here = pl.ds(pl.multiple_of(g * ROWS, ROWS), ROWS)

        def emit(which, matrix):
            for a in range(NVAR):
                for b in range(NVAR):
                    out[entry(which, a, b), here] = matrix[NVAR * a + b]

        def store_p(i, p):
            for k in range(NVAR * NVAR):
                held[i, k] = p[k]

        compose_lines(
            cells,
            lambda i, a, b: lower[a, b, i, here],
            lambda i, a, b: upper[a, b, i, here],
            store_p,
            lambda i: [held[i, k] for k in range(NVAR * NVAR)],
            emit,
        )
        return 0

    lax.fori_loop(0, rows // ROWS, group, 0)


def compose_y_kernel(lower, upper, y_inverse_hbm, out, y_inverse, held, semaphores):
    load = pltpu.make_async_copy(y_inverse_hbm, y_inverse, semaphores.at[0])
    load.start()
    cells_y = lower.shape[1]

    def emit(which, matrix):
        for a in range(NVAR):
            for b in range(NVAR):
                out[entry(which, a, b)] = matrix[NVAR * a + b]

    def store_p(i, p):
        for k in range(NVAR * NVAR):
            held[i, k] = p[k]

    compose_lines(
        cells_y,
        lambda j, a, b: lower[NVAR * a + b, j],
        lambda j, a, b: upper[NVAR * a + b, j],
        store_p,
        lambda i: [held[i, k] for k in range(NVAR * NVAR)],
        emit,
    )
    load.wait()


def local_x_kernel(
    field, forcing, x_pair, x_cross, y_pair, y_cross, inverse, lower, upper, _,
    reduced, source_out, padded, held,
):
    cells, rows, lanes = field.shape[1:]
    zero = jnp.zeros((rows, lanes), F32)
    middle = pl.ds(ROWS, rows)
    for c in range(NVAR):
        for i in range(cells):
            padded[c, i + 2, middle] = field[c, i]

    def y_before(value):
        for c in range(NVAR):
            for k in range(2):
                for i in range(cells):
                    padded[c, i + 2, ROWS - 2 + k] = value(c, k, i)

    def y_after(value):
        for c in range(NVAR):
            for k in range(2):
                for i in range(cells):
                    padded[c, i + 2, ROWS + rows + k] = value(c, k, i)

    def x_before(value):
        for c in range(NVAR):
            for k in range(2):
                padded[c, k, middle] = value(c, k)

    def x_after(value):
        for c in range(NVAR):
            for k in range(2):
                padded[c, cells + 2 + k, middle] = value(c, k)

    for axis, before, behind, pair, cross, empty in (
        ("px", x_before, x_after, lambda *k: x_pair[k], x_cross, jnp.zeros((rows, lanes), F32)),
        ("py", y_before, y_after, lambda *k: y_pair[k], y_cross, jnp.zeros((lanes,), F32)),
    ):
        at, count = lax.axis_index(axis), lax.axis_size(axis)

        @pl.when(bit(axis, 0) == 0)
        def _(before=before, behind=behind, pair=pair, cross=cross):
            before(lambda *k: cross[k])
            behind(pair)

        @pl.when(bit(axis, 0) == 1)
        def _(before=before, behind=behind, pair=pair, cross=cross):
            before(pair)
            behind(lambda *k: cross[k])

        @pl.when(at == 0)
        def _(before=before, empty=empty):
            before(lambda *k: empty)

        @pl.when(at == count - 1)
        def _(behind=behind, empty=empty):
            behind(lambda *k: empty)

    def right_side(i):
        out = []
        for c in range(NVAR):
            centre = padded[c, i + 2, middle]
            along_x = (
                padded[c, i, middle] - 4.0 * padded[c, i + 1, middle] + 6.0 * centre
                - 4.0 * padded[c, i + 3, middle] + padded[c, i + 4, middle]
            )
            along_y = (
                padded[c, i + 2, pl.ds(ROWS - 2, rows)]
                - 4.0 * padded[c, i + 2, pl.ds(ROWS - 1, rows)]
                + 6.0 * centre
                - 4.0 * padded[c, i + 2, pl.ds(ROWS + 1, rows)]
                + padded[c, i + 2, pl.ds(ROWS + 2, rows)]
            )
            out.append(forcing[c, i] - DISSIPATION * (along_x + along_y))
        return out

    def forward(i, v):
        s = matvec(lambda a, b: inverse[a, b, i], right_side(i))
        for c in range(NVAR):
            source_out[c, i] = s[c]
        v = minus(s, matvec(lambda a, b: lower[a, b, i], list(v)))
        for c in range(NVAR):
            held[c, i] = v[c]
        return tuple(v)

    v = lax.fori_loop(0, cells, forward, (zero,) * NVAR, unroll=True)
    for c in range(NVAR):
        reduced[0, c] = v[c]

    def backward(k, w):
        i = cells - 1 - k
        product = matvec(lambda a, b: upper[a, b, i], list(w))
        return tuple(held[c, i] - product[c] for c in range(NVAR))

    w = lax.fori_loop(0, cells, backward, (zero,) * NVAR, unroll=True)
    for c in range(NVAR):
        reduced[1, c] = w[c]


def vec(ref, which):
    return [ref[which, c] for c in range(NVAR)]


def entry(which, a, b):
    return (which * NVAR + a) * NVAR + b


def block(matrices, which, rows=slice(None)):
    return lambda a, b: matrices[entry(which, a, b), rows]


def whole(load):
    return [load(a, b) for a in range(NVAR) for b in range(NVAR)]


def in_order(axis, level, radix, bundles, then):
    place = (lax.axis_index(axis) >> level) & (radix - 1)
    for q in range(radix):

        @pl.when(place == q)
        def _(q=q):
            then(q, [bundles[m ^ q] for m in range(radix)])


def begin_kernel(cells, rows, field_hbm, x_lower_hbm, x_upper_hbm, y_lower_hbm, y_upper_hbm,
                 y_pair, y_cross, x_pair, x_cross, x_out, field, x_lower, x_upper, y_lower, y_upper,
                 held, semaphores):
    loads = [(field_hbm, field), (x_lower_hbm, x_lower), (x_upper_hbm, x_upper)]
    for source, target in ((y_lower_hbm, y_lower), (y_upper_hbm, y_upper)):
        for x in range(cells):
            loads.append((source.at[:, pl.ds(x * rows, rows), :], target.at[:, :, x, :]))
    copies = [
        pltpu.make_async_copy(source, target, semaphores.at[k])
        for k, (source, target) in enumerate(loads)
    ]
    for copy in copies:
        copy.start()
    copies[0].wait()

    def y_layers(out, j):
        for c in range(NVAR):
            for k in range(2):
                out[c, k] = field[c, pl.ds(j + k, cells, stride=rows), :]

    def x_layers(out, i):
        for c in range(NVAR):
            for k in range(2):
                out[c, k] = field[c, pl.ds((i + k) * rows, rows), :]

    @pl.when(bit("py", 0) == 0)
    def _():
        y_layers(y_pair, rows - 2)
        y_layers(y_cross, 0)

    @pl.when(bit("py", 0) == 1)
    def _():
        y_layers(y_pair, 0)
        y_layers(y_cross, rows - 2)

    @pl.when(bit("px", 0) == 0)
    def _():
        x_layers(x_pair, cells - 2)
        x_layers(x_cross, 0)

    @pl.when(bit("px", 0) == 1)
    def _():
        x_layers(x_pair, 0)
        x_layers(x_cross, cells - 2)

    copies[1].wait()
    copies[2].wait()
    compose_x(x_lower, x_upper, x_out, held)
    for copy in copies[3:]:
        copy.wait()


def grouped(refs, radix):
    return list(zip(refs[:radix], refs[radix : 2 * radix], strict=True))


def inflows(group, f):
    out = [f]
    for matrices, vectors in group:
        a = vec(vectors, 0)
        f = a if f is None else plus(matvec(block(matrices, 0), f), a)
        out.append(f)
    return out


def outflow(stretch, f, b):
    matrices, vectors = stretch
    out = vec(vectors, 1)
    if f is not None:
        out = plus(out, matvec(block(matrices, 2), f))
    if b is not None:
        out = plus(out, matvec(block(matrices, 1), b))
    return out


def join_vectors_kernel(axis, level, radix, last, *refs):
    out = refs[-1]

    def union_a(group):
        return inflows(group, None)[-1]

    def union_c(group):
        f, b = inflows(group[:-1], None), None
        for k in reversed(range(radix)):
            b = outflow(group[k], f[k], b)
        return b

    def then(q, group):
        if not last:
            for which, values in enumerate((union_a(group), union_c(group))):
                for k in range(NVAR):
                    out[which, k] = values[k]
            return

        for side, union in enumerate((union_a, union_c)):

            @pl.when(bit(axis, level + radix.bit_length() - 1) == side)
            def _(union=union):
                for k, value in enumerate(union(group)):
                    out[k] = value

    in_order(axis, level, radix, grouped(refs, radix), then)


def piece_of(axis, k):
    for piece, size in enumerate(PIECES[axis]):
        if k < size:
            return piece, k
        k -= size


def join_matrices_kernel(axis, level, radix, last, *refs):
    bundles, outs = refs[:radix], refs[radix:]
    lines = outs[0].shape[-2]

    def then(q, group):
        def register(g, _):
            here = pl.ds(pl.multiple_of(g * ROWS, ROWS), ROWS)
            at = lambda m, which: block(m, which, here)

            def emit(which, matrix):
                for k, value in enumerate(matrix):
                    if last:
                        piece, at_k = piece_of(axis, k)
                        outs[piece][at_k, here] = value
                    else:
                        outs[0][which * NVAR * NVAR + k, here] = value

            f = [None, whole(at(group[0], 0))]
            for m in group[1:-1]:
                f.append(matmat(at(m, 0), f[-1]))
            if not last:
                emit(0, matmat(at(group[-1], 0), f[-1]))
                r = whole(at(group[-1], 1))
                for m in reversed(group[:-1]):
                    r = matmat(at(m, 1), r)
                emit(1, r)
            c = matmat(at(group[-1], 2), f[-1])
            for k in reversed(range(1, radix - 1)):
                c = plus(matmat(at(group[k], 1), c), matmat(at(group[k], 2), f[k]))
            emit(2, plus(matmat(at(group[0], 1), c), whole(at(group[0], 2))))
            return 0

        lax.fori_loop(0, lines // ROWS, register, 0)

    wanted = bit(axis, level + radix.bit_length() - 1) == 1 if last else True

    @pl.when(wanted)
    def _():
        in_order(axis, level, radix, bundles, then)


def descend(axis, radices, refs, f_ref, b_ref):
    sizes = [2 * r for r in radices[:-1]]
    levels = [sum(r.bit_length() - 1 for r in radices[:t]) for t in range(len(radices))]
    *c_pieces, own, got = refs[sum(sizes) : descend_count(axis, radices)]
    shape = f_ref.shape[1:]

    def got_c(a, b):
        piece, at_k = piece_of(axis, NVAR * a + b)
        return c_pieces[piece][at_k]

    @pl.when(bit(axis, levels[-1]) == 0)
    def _():
        through = matvec(got_c, [own[k] for k in range(NVAR)])
        for k in range(NVAR):
            f_ref[k] = jnp.zeros(shape, F32)
            b_ref[k] = through[k] + got[k]

    @pl.when(bit(axis, levels[-1]) == 1)
    def _():
        for k in range(NVAR):
            f_ref[k] = got[k]
            b_ref[k] = jnp.zeros(shape, F32)

    for t in reversed(range(len(radices) - 1)):
        radix, first = radices[t], sum(sizes[:t])

        def then(q, group, radix=radix):
            f = inflows(group[:-1], [f_ref[k] for k in range(NVAR)])
            b = [b_ref[k] for k in range(NVAR)]
            for k in reversed(range(q + 1, radix)):
                b = outflow(group[k], f[k], b)
            for k in range(NVAR):
                f_ref[k] = f[q][k]
                b_ref[k] = b[k]

        here = grouped(refs[first : first + sizes[t]], radix)
        in_order(axis, levels[t], radix, here, then)


def descend_count(axis, radices):
    return sum(2 * r for r in radices[:-1]) + len(PIECES[axis]) + 2


def middle_kernel(radices, *rest):
    (source, x_lower, x_upper, y_inverse, y_lower, y_upper,
     reduced, y_source, f_ref, b_ref, held) = rest[descend_count("px", radices) :]
    cells, rows = source.shape[1:3]
    descend("px", radices, rest, f_ref, b_ref)

    def forward(i, v):
        product = matvec(lambda a, b: x_lower[a, b, i], list(v))
        v = [source[c, i] - product[c] for c in range(NVAR)]
        for c in range(NVAR):
            held[c, pl.ds(pl.multiple_of(i * rows, rows), rows)] = v[c]
        return tuple(v)

    lax.fori_loop(0, cells, forward, tuple(f_ref[k] for k in range(NVAR)), unroll=True)

    def backward(k, w):
        i = cells - 1 - k
        here = pl.ds(pl.multiple_of(i * rows, rows), rows)
        product = matvec(lambda a, b: x_upper[a, b, i], list(w))
        w = [held[c, here] - product[c] for c in range(NVAR)]
        s = matvec(lambda a, b: y_inverse[a, b, here], w)
        for c in range(NVAR):
            y_source[c, here] = s[c]
        return tuple(w)

    lax.fori_loop(0, cells, backward, tuple(b_ref[k] for k in range(NVAR)), unroll=True)

    def line(j):
        return pl.ds(j, cells, stride=rows)

    zero = jnp.zeros((cells, source.shape[3]), F32)

    def y_forward(j, v):
        product = matvec(lambda a, b: y_lower[NVAR * a + b, j], list(v))
        v = [y_source[c, line(j), :] - product[c] for c in range(NVAR)]
        for c in range(NVAR):
            held[c, pl.ds(pl.multiple_of(j * cells, cells), cells)] = v[c]
        return tuple(v)

    v = lax.fori_loop(0, rows, y_forward, (zero,) * NVAR, unroll=True)

    def y_backward(k, w):
        j = rows - 1 - k
        product = matvec(lambda a, b: y_upper[NVAR * a + b, j], list(w))
        here = pl.ds(pl.multiple_of(j * cells, cells), cells)
        return tuple(held[c, here] - product[c] for c in range(NVAR))

    w = lax.fori_loop(0, rows, y_backward, (zero,) * NVAR, unroll=True)
    for c in range(NVAR):
        reduced[0, c] = v[c]
        reduced[1, c] = w[c]


def end_kernel(radices, cells, rows, *rest):
    first = descend_count("py", radices)
    y_source, y_lower, y_upper, out, f_ref, b_ref, held = rest[first:]
    descend("py", radices, rest, f_ref, b_ref)

    def line(j):
        return pl.ds(j, cells, stride=rows)

    def forward(j, v):
        product = matvec(lambda a, b: y_lower[NVAR * a + b, j], list(v))
        v = [y_source[c, line(j), :] - product[c] for c in range(NVAR)]
        for c in range(NVAR):
            held[c, pl.ds(pl.multiple_of(j * cells, cells), cells)] = v[c]
        return tuple(v)

    lax.fori_loop(0, rows, forward, tuple(f_ref[k] for k in range(NVAR)), unroll=True)

    def backward(k, w):
        j = rows - 1 - k
        here = pl.ds(pl.multiple_of(j * cells, cells), cells)
        product = matvec(lambda a, b: y_upper[NVAR * a + b, j], list(w))
        w = [held[c, here] - product[c] for c in range(NVAR)]
        for c in range(NVAR):
            out[c, line(j), :] = w[c]
        return tuple(w)

    lax.fori_loop(0, rows, backward, tuple(b_ref[k] for k in range(NVAR)), unroll=True)


def radices_of(count):
    out, rest = [], count // 2
    while rest > 1:
        out.append(4 if rest % 4 == 0 else 2)
        rest //= out[-1]
    return out + [2]


def per_device(field, forcing, x_inverse, x_lower, x_upper, y_inverse, y_lower, y_upper):
    cells, rows, lanes = field.shape[1:]
    x_radices, y_radices = radices_of(lax.axis_size("px")), radices_of(lax.axis_size("py"))

    def swap(value, axis, step):
        pairs = [(i, i ^ step) for i in range(lax.axis_size(axis))]
        return lax.ppermute(value, axis, pairs)

    def across(value, axis):
        n = lax.axis_size(axis)
        pairs = [(i, (i + 1) % n) for i in range(1, n, 2)]
        if axis == "px":
            return lax.ppermute(value, axis, pairs + [(j, i) for i, j in pairs])
        swaps = []
        for x in range(lax.axis_size("px")):
            inner = [(x * n + i, x * n + j) for i, j in pairs[:-1]]
            swaps += inner + [(j, i) for i, j in inner]
            swaps += [(x * n + i, (x ^ 1) * n + i) for i in (0, n - 1)]
        return lax.ppermute(value, ("px", "py"), swaps)

    flat = lambda m: m.reshape(m.shape[:-3] + (cells * rows, lanes))
    y_inverse = flat(y_inverse)

    every = NVAR * NVAR
    y_pair, y_cross, x_pair, x_cross, x_m, field, x_lower, x_upper, y_lower, y_upper = call(
        functools.partial(begin_kernel, cells, rows), "begin",
        [(NVAR, 2, cells, lanes)] * 2 + [(NVAR, 2, rows, lanes)] * 2
        + [(MATRICES, rows, lanes), (NVAR, cells * rows, lanes)] + [x_lower.shape] * 2
        + [(every, rows, cells, lanes)] * 2,
        [], [(cells, every, ROWS, lanes)],
        from_hbm=[flat(field), x_lower, x_upper]
        + [m.reshape(every, cells * rows, lanes) for m in (y_lower, y_upper)],
        copies=3 + 2 * cells,
    )
    field = field.reshape(NVAR, cells, rows, lanes)
    y_cross, x_cross = across(y_cross, "py"), across(x_cross, "px")
    y_pair, x_pair = swap(y_pair, "py", 1), swap(x_pair, "px", 1)
    halos = (x_pair, x_cross, y_pair, y_cross)

    def exchange(axis, radices, own_m, got_m, own_v, rest):
        operands, level = [], 0
        for t, radix in enumerate(radices[:-1]):
            last = t == len(radices) - 2
            settings = (axis, level, radix, last)
            got_v = [swap(own_v, axis, k << level) for k in range(1, radix)]
            lines = own_m.shape[1:]
            sizes = PIECES[axis] if last else (MATRICES,)
            next_m = call(functools.partial(join_matrices_kernel, *settings), "join_matrices",
                          [(size, *lines) for size in sizes], [own_m, *got_m])
            next_m = list(next_m) if len(sizes) > 1 else [next_m]
            next_level = level + radix.bit_length() - 1
            next_got = [swap(m, axis, k << next_level)
                        for k in range(1, radices[t + 1]) for m in next_m]
            count = len(operands)
            operands += [own_m, *got_m, own_v, *got_v]
            held = hold(operands + rest)
            operands, rest = held[: len(operands)], held[len(operands) :]
            own_v = call(functools.partial(join_vectors_kernel, *settings), "join_vectors",
                         [own_v.shape[last:]], operands[count:])
            if not last:
                next_got = hold(next_got, own_v)
            own_m, got_m, level = next_m[0], next_got, next_level
        operands += [*got_m, own_v, swap(own_v, axis, 1 << level)]
        held = hold(operands + rest)
        return held[: len(operands)], held[len(operands) :]

    y_m, y_inverse = call(
        compose_y_kernel, "compose_y", [(MATRICES, cells, lanes), y_inverse.shape],
        [y_lower, y_upper], [(rows, every, cells, lanes)], from_hbm=[y_inverse], copies=1,
    )
    y_got = [swap(y_m, "py", k) for k in range(1, y_radices[0])]
    reduced, source = call(
        local_x_kernel, "local_x",
        [(VX, NVAR, rows, lanes), (NVAR, cells, rows, lanes)],
        [field, forcing, *halos, x_inverse, x_lower, x_upper, y_m],
        [(NVAR, cells + 4, rows + 2 * ROWS, lanes), (NVAR, cells, rows, lanes)],
    )
    x_got = [swap(x_m, "px", k) for k in range(1, x_radices[0])]
    rest = [source, x_lower, x_upper, y_inverse, y_lower, y_upper]
    operands, rest = exchange("px", x_radices, x_m, x_got, reduced, rest)
    reduced, source = call(
        functools.partial(middle_kernel, x_radices), "middle",
        [(2, NVAR, cells, lanes), (NVAR, cells * rows, lanes)],
        operands + rest,
        [(NVAR, rows, lanes), (NVAR, rows, lanes), (NVAR, cells * rows, lanes)],
    )
    y_m, *y_got = hold([y_m, *y_got], reduced)
    operands, rest = exchange(
        "py", y_radices, y_m, y_got, reduced, [source, *rest[-2:]]
    )
    out = call(
        functools.partial(end_kernel, y_radices, cells, rows), "end",
        [(NVAR, cells * rows, lanes)],
        operands + rest,
        [(NVAR, cells, lanes), (NVAR, cells, lanes), (NVAR, cells * rows, lanes)],
        result_in_hbm=True,
    )
    return out.reshape(NVAR, cells, rows, lanes)


def solution(mesh):
    cell = P(None, "px", "py", None)
    blocks = P(None, None, "px", "py", None)
    return jax.shard_map(
        per_device,
        mesh=mesh,
        in_specs=(cell, cell) + (blocks,) * 6,
        out_specs=cell,
        check_vma=False,
    )
```

```python
import functools

import jax
import jax.numpy as jnp
from jax import lax
from jax.experimental import pallas as pl
from jax.experimental.pallas import tpu as pltpu
from jax.sharding import PartitionSpec as P

DISSIPATION = 0.1
NVAR = 5
F32 = jnp.float32
ROWS = 8
UNROLL = 3
MATRICES = 3 * NVAR * NVAR
VX = 2
PIECES = {"px": (25,), "py": (13, 12)}
VMEM_BYTES = 12 * 1024 * 1024


def call(kernel, name, out_shapes, operands, scratch=(), result_in_hbm=False, from_hbm=(),
         copies=0):
    vmem = pl.BlockSpec(memory_space=pltpu.VMEM)
    make = jax.ShapeDtypeStruct if result_in_hbm else pltpu.VMEM
    shapes = [make(s, F32) for s in out_shapes]
    single = len(shapes) == 1
    operands = [pltpu.with_memory_space_constraint(x, pltpu.VMEM) for x in operands]
    outer = [pltpu.with_memory_space_constraint(x, pltpu.HBM) for x in from_hbm]
    semaphores = [pltpu.SemaphoreType.DMA((copies,))] if copies else []
    return pl.pallas_call(
        kernel,
        name=name,
        out_shape=shapes[0] if single else shapes,
        in_specs=[vmem] * len(operands) + [pl.BlockSpec(memory_space=pltpu.HBM)] * len(outer),
        out_specs=vmem if single else [vmem] * len(shapes),
        scratch_shapes=[pltpu.VMEM(s, F32) for s in scratch] + semaphores,
        compiler_params=pltpu.CompilerParams(vmem_limit_bytes=VMEM_BYTES),
    )(*operands, *outer)


def hold(arrays, *others):
    def nothing(*refs):
        pass

    operands = [pltpu.with_memory_space_constraint(x, pltpu.VMEM) for x in (*arrays, *others)]
    anywhere = pl.BlockSpec(memory_space=pl.ANY)
    held = pl.pallas_call(
        nothing,
        name="hold",
        out_shape=[pltpu.VMEM(x.shape, F32) for x in arrays],
        in_specs=[anywhere] * len(operands),
        out_specs=[anywhere] * len(arrays),
        input_output_aliases={k: k for k in range(len(arrays))},
        compiler_params=pltpu.CompilerParams(vmem_limit_bytes=1024 * 1024),
    )(*operands)
    return list(held)


def bit(axis, level):
    return (lax.axis_index(axis) >> level) & 1


def tree(terms):
    while len(terms) > 1:
        pairs = [terms[k] + terms[k + 1] for k in range(0, len(terms) - 1, 2)]
        terms = pairs + (terms[-1:] if len(terms) % 2 else [])
    return terms[0]


def matvec(load, vector):
    return [tree([load(a, b) * vector[b] for b in range(NVAR)]) for a in range(NVAR)]


def matmat(load, matrix):
    out = []
    for a in range(NVAR):
        row = [load(a, b) for b in range(NVAR)]
        for c in range(NVAR):
            out.append(tree([row[b] * matrix[NVAR * b + c] for b in range(NVAR)]))
    return out


def plus(left, right):
    return [p + q for p, q in zip(left, right, strict=True)]


def minus(left, right):
    return [p - q for p, q in zip(left, right, strict=True)]


def signed(matrix, length):
    return [-q for q in matrix] if length % 2 else list(matrix)


def compose_forward(length, lower_at, store_p, emit):
    first = whole(lambda a, b: lower_at(0, a, b))
    store_p(0, first)

    def forward(i, p):
        p = matmat(lambda a, b: lower_at(i, a, b), p)
        store_p(i, p)
        return tuple(p)

    last = lax.fori_loop(1, length, forward, tuple(first), unroll=UNROLL)
    emit(0, signed(last, length))


def compose_backward(length, upper_at, load_p, emit):
    def backward(k, carried):
        w, r = carried
        i = length - 1 - k
        here = whole(lambda a, b: upper_at(i, a, b))
        at = lambda a, b: here[NVAR * a + b]
        return tuple(plus(load_p(i), matmat(at, w))), tuple(matmat(at, r))

    w = tuple(load_p(length - 1))
    r = tuple(whole(lambda a, b: upper_at(length - 1, a, b)))
    w, r = lax.fori_loop(1, length, backward, (w, r), unroll=UNROLL)
    emit(1, signed(r, length))
    emit(2, [-q for q in w])


def compose_x(lower, upper, out, held, turn):
    cells, rows = lower.shape[2:4]

    def register(g):
        here = pl.ds(pl.multiple_of(g * ROWS, ROWS), ROWS)

        def emit(which, matrix):
            for k, value in enumerate(matrix):
                out[which * NVAR * NVAR + k, here] = value

        def store_p(i, p):
            for k in range(NVAR * NVAR):
                held[i, k, here] = p[k]

        load_p = lambda i: [held[i, k, here] for k in range(NVAR * NVAR)]
        return here, emit, store_p, load_p

    def forward(g, _):
        here, emit, store_p, _ = register(g)
        compose_forward(cells, lambda i, a, b: lower[a, b, i, here], store_p, emit)
        return 0

    def backward(g, _):
        here, emit, _, load_p = register(g)
        compose_backward(cells, lambda i, a, b: upper[a, b, i, here], load_p, emit)
        return 0

    lax.fori_loop(0, rows // ROWS, forward, 0)
    turn()
    lax.fori_loop(0, rows // ROWS, backward, 0)


def compose_y_kernel(lower, upper, y_inverse_hbm, out, y_inverse, held, semaphores):
    load = pltpu.make_async_copy(y_inverse_hbm, y_inverse, semaphores.at[0])
    load.start()
    cells_y = lower.shape[1]

    def emit(which, matrix):
        for a in range(NVAR):
            for b in range(NVAR):
                out[entry(which, a, b)] = matrix[NVAR * a + b]

    def store_p(i, p):
        for k in range(NVAR * NVAR):
            held[i, k] = p[k]

    at = lambda ref: lambda j, a, b: ref[NVAR * a + b, j]
    compose_forward(cells_y, at(lower), store_p, emit)
    compose_backward(
        cells_y, at(upper), lambda i: [held[i, k] for k in range(NVAR * NVAR)], emit
    )
    load.wait()


def local_x_kernel(
    field, forcing, x_pair, x_cross, y_pair, y_cross, inverse, lower, upper, _,
    reduced, source_out, padded, held,
):
    cells, rows, lanes = field.shape[1:]
    zero = jnp.zeros((rows, lanes), F32)
    middle = pl.ds(ROWS, rows)
    for c in range(NVAR):
        for i in range(cells):
            padded[c, i + 2, middle] = field[c, i]

    def y_before(value):
        for c in range(NVAR):
            for k in range(2):
                for i in range(cells):
                    padded[c, i + 2, ROWS - 2 + k] = value(c, k, i)

    def y_after(value):
        for c in range(NVAR):
            for k in range(2):
                for i in range(cells):
                    padded[c, i + 2, ROWS + rows + k] = value(c, k, i)

    def x_before(value):
        for c in range(NVAR):
            for k in range(2):
                padded[c, k, middle] = value(c, k)

    def x_after(value):
        for c in range(NVAR):
            for k in range(2):
                padded[c, cells + 2 + k, middle] = value(c, k)

    for axis, before, behind, pair, cross, empty in (
        ("px", x_before, x_after, lambda *k: x_pair[k], x_cross, jnp.zeros((rows, lanes), F32)),
        ("py", y_before, y_after, lambda *k: y_pair[k], y_cross, jnp.zeros((lanes,), F32)),
    ):
        at, count = lax.axis_index(axis), lax.axis_size(axis)

        @pl.when(bit(axis, 0) == 0)
        def _(before=before, behind=behind, pair=pair, cross=cross):
            before(lambda *k: cross[k])
            behind(pair)

        @pl.when(bit(axis, 0) == 1)
        def _(before=before, behind=behind, pair=pair, cross=cross):
            before(pair)
            behind(lambda *k: cross[k])

        @pl.when(at == 0)
        def _(before=before, empty=empty):
            before(lambda *k: empty)

        @pl.when(at == count - 1)
        def _(behind=behind, empty=empty):
            behind(lambda *k: empty)

    def right_side(i):
        out = []
        for c in range(NVAR):
            centre = padded[c, i + 2, middle]
            along_x = (
                padded[c, i, middle] - 4.0 * padded[c, i + 1, middle] + 6.0 * centre
                - 4.0 * padded[c, i + 3, middle] + padded[c, i + 4, middle]
            )
            along_y = (
                padded[c, i + 2, pl.ds(ROWS - 2, rows)]
                - 4.0 * padded[c, i + 2, pl.ds(ROWS - 1, rows)]
                + 6.0 * centre
                - 4.0 * padded[c, i + 2, pl.ds(ROWS + 1, rows)]
                + padded[c, i + 2, pl.ds(ROWS + 2, rows)]
            )
            out.append(forcing[c, i] - DISSIPATION * (along_x + along_y))
        return out

    def forward(i, v):
        s = matvec(lambda a, b: inverse[a, b, i], right_side(i))
        for c in range(NVAR):
            source_out[c, i] = s[c]
        v = minus(s, matvec(lambda a, b: lower[a, b, i], list(v)))
        for c in range(NVAR):
            held[c, i] = v[c]
        return tuple(v)

    v = lax.fori_loop(0, cells, forward, (zero,) * NVAR, unroll=True)
    for c in range(NVAR):
        reduced[0, c] = v[c]

    def backward(k, w):
        i = cells - 1 - k
        product = matvec(lambda a, b: upper[a, b, i], list(w))
        return tuple(held[c, i] - product[c] for c in range(NVAR))

    w = lax.fori_loop(0, cells, backward, (zero,) * NVAR, unroll=True)
    for c in range(NVAR):
        reduced[1, c] = w[c]


def vec(ref, which):
    return [ref[which, c] for c in range(NVAR)]


def entry(which, a, b):
    return (which * NVAR + a) * NVAR + b


def block(matrices, which, rows=slice(None)):
    return lambda a, b: matrices[entry(which, a, b), rows]


def whole(load):
    return [load(a, b) for a in range(NVAR) for b in range(NVAR)]


def in_order(axis, level, radix, bundles, then):
    place = (lax.axis_index(axis) >> level) & (radix - 1)
    for q in range(radix):

        @pl.when(place == q)
        def _(q=q):
            then(q, [bundles[m ^ q] for m in range(radix)])


def begin_kernel(cells, rows, field_hbm, x_lower_hbm, x_upper_hbm, y_lower_hbm, y_upper_hbm,
                 y_pair, y_cross, x_pair, x_cross, x_out, field, x_lower, x_upper, y_lower, y_upper,
                 held, semaphores):
    loads = [(field_hbm, field), (x_lower_hbm, x_lower), (x_upper_hbm, x_upper)]
    for source, target in ((y_lower_hbm, y_lower), (y_upper_hbm, y_upper)):
        for x in range(cells):
            loads.append((source.at[:, pl.ds(x * rows, rows), :], target.at[:, :, x, :]))
    copies = [
        pltpu.make_async_copy(source, target, semaphores.at[k])
        for k, (source, target) in enumerate(loads)
    ]
    for copy in copies:
        copy.start()
    copies[0].wait()

    def y_layers(out, j):
        for c in range(NVAR):
            for k in range(2):
                out[c, k] = field[c, pl.ds(j + k, cells, stride=rows), :]

    def x_layers(out, i):
        for c in range(NVAR):
            for k in range(2):
                out[c, k] = field[c, pl.ds((i + k) * rows, rows), :]

    @pl.when(bit("py", 0) == 0)
    def _():
        y_layers(y_pair, rows - 2)
        y_layers(y_cross, 0)

    @pl.when(bit("py", 0) == 1)
    def _():
        y_layers(y_pair, 0)
        y_layers(y_cross, rows - 2)

    @pl.when(bit("px", 0) == 0)
    def _():
        x_layers(x_pair, cells - 2)
        x_layers(x_cross, 0)

    @pl.when(bit("px", 0) == 1)
    def _():
        x_layers(x_pair, 0)
        x_layers(x_cross, cells - 2)

    copies[1].wait()
    compose_x(x_lower, x_upper, x_out, held, copies[2].wait)
    for copy in copies[3:]:
        copy.wait()


def grouped(refs, radix):
    return list(zip(refs[:radix], refs[radix : 2 * radix], strict=True))


def inflows(group, f):
    out = [f]
    for matrices, vectors in group:
        a = vec(vectors, 0)
        f = a if f is None else plus(matvec(block(matrices, 0), f), a)
        out.append(f)
    return out


def outflow(stretch, f, b):
    matrices, vectors = stretch
    out = vec(vectors, 1)
    if f is not None:
        out = plus(out, matvec(block(matrices, 2), f))
    if b is not None:
        out = plus(out, matvec(block(matrices, 1), b))
    return out


def join_vectors_kernel(axis, level, radix, last, *refs):
    out = refs[-1]

    def union_a(group):
        return inflows(group, None)[-1]

    def union_c(group):
        f, b = inflows(group[:-1], None), None
        for k in reversed(range(radix)):
            b = outflow(group[k], f[k], b)
        return b

    def then(q, group):
        if not last:
            for which, values in enumerate((union_a(group), union_c(group))):
                for k in range(NVAR):
                    out[which, k] = values[k]
            return

        for side, union in enumerate((union_a, union_c)):

            @pl.when(bit(axis, level + radix.bit_length() - 1) == side)
            def _(union=union):
                for k, value in enumerate(union(group)):
                    out[k] = value

    in_order(axis, level, radix, grouped(refs, radix), then)


def piece_of(axis, k):
    for piece, size in enumerate(PIECES[axis]):
        if k < size:
            return piece, k
        k -= size


def join_matrices_kernel(axis, level, radix, last, *refs):
    bundles, outs = refs[:radix], refs[radix:]
    lines = outs[0].shape[-2]

    def then(q, group):
        def register(g, _):
            here = pl.ds(pl.multiple_of(g * ROWS, ROWS), ROWS)
            at = lambda m, which: block(m, which, here)

            def emit(which, matrix):
                for k, value in enumerate(matrix):
                    if last:
                        piece, at_k = piece_of(axis, k)
                        outs[piece][at_k, here] = value
                    else:
                        outs[0][which * NVAR * NVAR + k, here] = value

            f = [None, whole(at(group[0], 0))]
            for m in group[1:-1]:
                f.append(matmat(at(m, 0), f[-1]))
            if not last:
                emit(0, matmat(at(group[-1], 0), f[-1]))
                r = whole(at(group[-1], 1))
                for m in reversed(group[:-1]):
                    r = matmat(at(m, 1), r)
                emit(1, r)
            c = matmat(at(group[-1], 2), f[-1])
            for k in reversed(range(1, radix - 1)):
                c = plus(matmat(at(group[k], 1), c), matmat(at(group[k], 2), f[k]))
            emit(2, plus(matmat(at(group[0], 1), c), whole(at(group[0], 2))))
            return 0

        lax.fori_loop(0, lines // ROWS, register, 0)

    wanted = bit(axis, level + radix.bit_length() - 1) == 1 if last else True

    @pl.when(wanted)
    def _():
        in_order(axis, level, radix, bundles, then)


def descend(axis, radices, refs, f_ref, b_ref):
    sizes = [2 * r for r in radices[:-1]]
    levels = [sum(r.bit_length() - 1 for r in radices[:t]) for t in range(len(radices))]
    *c_pieces, own, got = refs[sum(sizes) : descend_count(axis, radices)]
    shape = f_ref.shape[1:]

    def got_c(a, b):
        piece, at_k = piece_of(axis, NVAR * a + b)
        return c_pieces[piece][at_k]

    @pl.when(bit(axis, levels[-1]) == 0)
    def _():
        through = matvec(got_c, [own[k] for k in range(NVAR)])
        for k in range(NVAR):
            f_ref[k] = jnp.zeros(shape, F32)
            b_ref[k] = through[k] + got[k]

    @pl.when(bit(axis, levels[-1]) == 1)
    def _():
        for k in range(NVAR):
            f_ref[k] = got[k]
            b_ref[k] = jnp.zeros(shape, F32)

    for t in reversed(range(len(radices) - 1)):
        radix, first = radices[t], sum(sizes[:t])

        def then(q, group, radix=radix):
            f = inflows(group[:-1], [f_ref[k] for k in range(NVAR)])
            b = [b_ref[k] for k in range(NVAR)]
            for k in reversed(range(q + 1, radix)):
                b = outflow(group[k], f[k], b)
            for k in range(NVAR):
                f_ref[k] = f[q][k]
                b_ref[k] = b[k]

        here = grouped(refs[first : first + sizes[t]], radix)
        in_order(axis, levels[t], radix, here, then)


def descend_count(axis, radices):
    return sum(2 * r for r in radices[:-1]) + len(PIECES[axis]) + 2


def middle_kernel(radices, *rest):
    (source, x_lower, x_upper, y_inverse, y_lower, y_upper,
     reduced, y_source, f_ref, b_ref, held) = rest[descend_count("px", radices) :]
    cells, rows = source.shape[1:3]
    descend("px", radices, rest, f_ref, b_ref)

    def forward(i, v):
        product = matvec(lambda a, b: x_lower[a, b, i], list(v))
        v = [source[c, i] - product[c] for c in range(NVAR)]
        for c in range(NVAR):
            held[c, pl.ds(pl.multiple_of(i * rows, rows), rows)] = v[c]
        return tuple(v)

    lax.fori_loop(0, cells, forward, tuple(f_ref[k] for k in range(NVAR)), unroll=True)

    def backward(k, w):
        i = cells - 1 - k
        here = pl.ds(pl.multiple_of(i * rows, rows), rows)
        product = matvec(lambda a, b: x_upper[a, b, i], list(w))
        w = [held[c, here] - product[c] for c in range(NVAR)]
        s = matvec(lambda a, b: y_inverse[a, b, here], w)
        for c in range(NVAR):
            y_source[c, here] = s[c]
        return tuple(w)

    lax.fori_loop(0, cells, backward, tuple(b_ref[k] for k in range(NVAR)), unroll=True)

    def line(j):
        return pl.ds(j, cells, stride=rows)

    zero = jnp.zeros((cells, source.shape[3]), F32)

    def y_forward(j, v):
        product = matvec(lambda a, b: y_lower[NVAR * a + b, j], list(v))
        v = [y_source[c, line(j), :] - product[c] for c in range(NVAR)]
        for c in range(NVAR):
            held[c, pl.ds(pl.multiple_of(j * cells, cells), cells)] = v[c]
        return tuple(v)

    v = lax.fori_loop(0, rows, y_forward, (zero,) * NVAR, unroll=True)

    def y_backward(k, w):
        j = rows - 1 - k
        product = matvec(lambda a, b: y_upper[NVAR * a + b, j], list(w))
        here = pl.ds(pl.multiple_of(j * cells, cells), cells)
        return tuple(held[c, here] - product[c] for c in range(NVAR))

    w = lax.fori_loop(0, rows, y_backward, (zero,) * NVAR, unroll=True)
    for c in range(NVAR):
        reduced[0, c] = v[c]
        reduced[1, c] = w[c]


def end_kernel(radices, cells, rows, *rest):
    first = descend_count("py", radices)
    y_source, y_lower, y_upper, out, f_ref, b_ref, held = rest[first:]
    descend("py", radices, rest, f_ref, b_ref)

    def line(j):
        return pl.ds(j, cells, stride=rows)

    def forward(j, v):
        product = matvec(lambda a, b: y_lower[NVAR * a + b, j], list(v))
        v = [y_source[c, line(j), :] - product[c] for c in range(NVAR)]
        for c in range(NVAR):
            held[c, pl.ds(pl.multiple_of(j * cells, cells), cells)] = v[c]
        return tuple(v)

    lax.fori_loop(0, rows, forward, tuple(f_ref[k] for k in range(NVAR)), unroll=True)

    def backward(k, w):
        j = rows - 1 - k
        here = pl.ds(pl.multiple_of(j * cells, cells), cells)
        product = matvec(lambda a, b: y_upper[NVAR * a + b, j], list(w))
        w = [held[c, here] - product[c] for c in range(NVAR)]
        for c in range(NVAR):
            out[c, line(j), :] = w[c]
        return tuple(w)

    lax.fori_loop(0, rows, backward, tuple(b_ref[k] for k in range(NVAR)), unroll=True)


def radices_of(count):
    out, rest = [], count // 2
    while rest > 1:
        out.append(4 if rest % 4 == 0 else 2)
        rest //= out[-1]
    return out + [2]


def per_device(field, forcing, x_inverse, x_lower, x_upper, y_inverse, y_lower, y_upper):
    cells, rows, lanes = field.shape[1:]
    x_radices, y_radices = radices_of(lax.axis_size("px")), radices_of(lax.axis_size("py"))

    def swap(value, axis, step):
        pairs = [(i, i ^ step) for i in range(lax.axis_size(axis))]
        return lax.ppermute(value, axis, pairs)

    def across(value, axis):
        n = lax.axis_size(axis)
        pairs = [(i, (i + 1) % n) for i in range(1, n, 2)]
        if axis == "px":
            return lax.ppermute(value, axis, pairs + [(j, i) for i, j in pairs])
        swaps = []
        for x in range(lax.axis_size("px")):
            inner = [(x * n + i, x * n + j) for i, j in pairs[:-1]]
            swaps += inner + [(j, i) for i, j in inner]
            swaps += [(x * n + i, (x ^ 1) * n + i) for i in (0, n - 1)]
        return lax.ppermute(value, ("px", "py"), swaps)

    flat = lambda m: m.reshape(m.shape[:-3] + (cells * rows, lanes))
    y_inverse = flat(y_inverse)

    every = NVAR * NVAR
    y_pair, y_cross, x_pair, x_cross, x_m, field, x_lower, x_upper, y_lower, y_upper = call(
        functools.partial(begin_kernel, cells, rows), "begin",
        [(NVAR, 2, cells, lanes)] * 2 + [(NVAR, 2, rows, lanes), (NVAR, 6, rows, lanes)]
        + [(MATRICES, rows, lanes), (NVAR, cells * rows, lanes)] + [x_lower.shape] * 2
        + [(every, rows, cells, lanes)] * 2,
        [], [(cells, every, rows, lanes)],
        from_hbm=[flat(field), x_lower, x_upper]
        + [m.reshape(every, cells * rows, lanes) for m in (y_lower, y_upper)],
        copies=3 + 2 * cells,
    )
    field = field.reshape(NVAR, cells, rows, lanes)
    y_cross, x_cross = across(y_cross, "py"), across(x_cross, "px")
    y_pair, x_pair = swap(y_pair, "py", 1), swap(x_pair, "px", 1)
    halos = (x_pair, x_cross, y_pair, y_cross)

    def exchange(axis, radices, own_m, got_m, own_v, rest):
        operands, level = [], 0
        for t, radix in enumerate(radices[:-1]):
            last = t == len(radices) - 2
            settings = (axis, level, radix, last)
            got_v = [swap(own_v, axis, k << level) for k in range(1, radix)]
            lines = own_m.shape[1:]
            sizes = PIECES[axis] if last else (MATRICES,)
            next_m = call(functools.partial(join_matrices_kernel, *settings), "join_matrices",
                          [(size, *lines) for size in sizes], [own_m, *got_m])
            next_m = list(next_m) if len(sizes) > 1 else [next_m]
            next_level = level + radix.bit_length() - 1
            next_got = [swap(m, axis, k << next_level)
                        for k in range(1, radices[t + 1]) for m in next_m]
            count = len(operands)
            operands += [own_m, *got_m, own_v, *got_v]
            held = hold(operands + rest)
            operands, rest = held[: len(operands)], held[len(operands) :]
            own_v = call(functools.partial(join_vectors_kernel, *settings), "join_vectors",
                         [own_v.shape[last:]], operands[count:])
            if not last:
                next_got = hold(next_got, own_v)
            own_m, got_m, level = next_m[0], next_got, next_level
        operands += [*got_m, own_v, swap(own_v, axis, 1 << level)]
        held = hold(operands + rest)
        return held[: len(operands)], held[len(operands) :]

    y_m, y_inverse = call(
        compose_y_kernel, "compose_y", [(MATRICES, cells, lanes), y_inverse.shape],
        [y_lower, y_upper], [(rows, every, cells, lanes)], from_hbm=[y_inverse], copies=1,
    )
    y_got = [swap(y_m, "py", k) for k in range(1, y_radices[0])]
    reduced, source = call(
        local_x_kernel, "local_x",
        [(VX, NVAR, rows, lanes), (NVAR, cells, rows, lanes)],
        [field, forcing, *halos, x_inverse, x_lower, x_upper, y_m],
        [(NVAR, cells + 4, rows + 2 * ROWS, lanes), (NVAR, cells, rows, lanes)],
    )
    x_got = [swap(x_m, "px", k) for k in range(1, x_radices[0])]
    rest = [source, x_lower, x_upper, y_inverse, y_lower, y_upper]
    operands, rest = exchange("px", x_radices, x_m, x_got, reduced, rest)
    reduced, source = call(
        functools.partial(middle_kernel, x_radices), "middle",
        [(2, NVAR, cells, lanes), (NVAR, cells * rows, lanes)],
        operands + rest,
        [(NVAR, rows, lanes), (NVAR, rows, lanes), (NVAR, cells * rows, lanes)],
    )
    y_m, *y_got = hold([y_m, *y_got], reduced)
    operands, rest = exchange(
        "py", y_radices, y_m, y_got, reduced, [source, *rest[-2:]]
    )
    out = call(
        functools.partial(end_kernel, y_radices, cells, rows), "end",
        [(NVAR, cells * rows, lanes)],
        operands + rest,
        [(NVAR, cells, lanes), (NVAR, cells, lanes), (NVAR, cells * rows, lanes)],
        result_in_hbm=True,
    )
    return out.reshape(NVAR, cells, rows, lanes)


def solution(mesh):
    cell = P(None, "px", "py", None)
    blocks = P(None, None, "px", "py", None)
    return jax.shard_map(
        per_device,
        mesh=mesh,
        in_specs=(cell, cell) + (blocks,) * 6,
        out_specs=cell,
        check_vma=False,
    )
```

```python
import functools

import jax
import jax.numpy as jnp
from jax import lax
from jax.experimental import pallas as pl
from jax.experimental.pallas import tpu as pltpu
from jax.sharding import PartitionSpec as P

DISSIPATION = 0.1
NVAR = 5
F32 = jnp.float32
ROWS = 8
UNROLL = 3
MATRICES = 3 * NVAR * NVAR
VX = 2
SCALED = ("py",)
PIECES = {"px": (25,), "py": (13, 13)}
VMEM_BYTES = 12 * 1024 * 1024


def call(kernel, name, out_shapes, operands, scratch=(), result_in_hbm=False, from_hbm=(),
         copies=0):
    vmem = pl.BlockSpec(memory_space=pltpu.VMEM)
    make = jax.ShapeDtypeStruct if result_in_hbm else pltpu.VMEM
    shapes = [make(s, F32) for s in out_shapes]
    single = len(shapes) == 1
    operands = [pltpu.with_memory_space_constraint(x, pltpu.VMEM) for x in operands]
    outer = [pltpu.with_memory_space_constraint(x, pltpu.HBM) for x in from_hbm]
    semaphores = [pltpu.SemaphoreType.DMA((copies,))] if copies else []
    return pl.pallas_call(
        kernel,
        name=name,
        out_shape=shapes[0] if single else shapes,
        in_specs=[vmem] * len(operands) + [pl.BlockSpec(memory_space=pltpu.HBM)] * len(outer),
        out_specs=vmem if single else [vmem] * len(shapes),
        scratch_shapes=[pltpu.VMEM(s, F32) for s in scratch] + semaphores,
        compiler_params=pltpu.CompilerParams(vmem_limit_bytes=VMEM_BYTES),
    )(*operands, *outer)


def hold(arrays, *others):
    def nothing(*refs):
        pass

    operands = [pltpu.with_memory_space_constraint(x, pltpu.VMEM) for x in (*arrays, *others)]
    anywhere = pl.BlockSpec(memory_space=pl.ANY)
    held = pl.pallas_call(
        nothing,
        name="hold",
        out_shape=[pltpu.VMEM(x.shape, F32) for x in arrays],
        in_specs=[anywhere] * len(operands),
        out_specs=[anywhere] * len(arrays),
        input_output_aliases={k: k for k in range(len(arrays))},
        compiler_params=pltpu.CompilerParams(vmem_limit_bytes=1024 * 1024),
    )(*operands)
    return list(held)


def bit(axis, level):
    return (lax.axis_index(axis) >> level) & 1


def tree(terms):
    while len(terms) > 1:
        pairs = [terms[k] + terms[k + 1] for k in range(0, len(terms) - 1, 2)]
        terms = pairs + (terms[-1:] if len(terms) % 2 else [])
    return terms[0]


def matvec(load, vector):
    return [tree([load(a, b) * vector[b] for b in range(NVAR)]) for a in range(NVAR)]


def matmat(load, matrix):
    out = []
    for a in range(NVAR):
        row = [load(a, b) for b in range(NVAR)]
        for c in range(NVAR):
            out.append(tree([row[b] * matrix[NVAR * b + c] for b in range(NVAR)]))
    return out


def plus(left, right):
    return [p + q for p, q in zip(left, right, strict=True)]


def minus(left, right):
    return [p - q for p, q in zip(left, right, strict=True)]


def signed(matrix, length):
    return [-q for q in matrix] if length % 2 else list(matrix)


def compose_forward(length, lower_at, store_p, emit):
    first = whole(lambda a, b: lower_at(0, a, b))
    store_p(0, first)

    def forward(i, p):
        p = matmat(lambda a, b: lower_at(i, a, b), p)
        store_p(i, p)
        return tuple(p)

    last = lax.fori_loop(1, length, forward, tuple(first), unroll=UNROLL)
    emit(0, signed(last, length))


def compose_backward(length, upper_at, load_p, emit):
    def backward(k, carried):
        w, r = carried
        i = length - 1 - k
        here = whole(lambda a, b: upper_at(i, a, b))
        at = lambda a, b: here[NVAR * a + b]
        return tuple(plus(load_p(i), matmat(at, w))), tuple(matmat(at, r))

    w = tuple(load_p(length - 1))
    r = tuple(whole(lambda a, b: upper_at(length - 1, a, b)))
    w, r = lax.fori_loop(1, length, backward, (w, r), unroll=UNROLL)
    emit(1, signed(r, length))
    emit(2, [-q for q in w])


def compose_x(lower, upper, out, held, turn):
    cells, rows = lower.shape[2:4]

    def register(g):
        here = pl.ds(pl.multiple_of(g * ROWS, ROWS), ROWS)

        def emit(which, matrix):
            for k, value in enumerate(matrix):
                out[which * NVAR * NVAR + k, here] = value

        def store_p(i, p):
            for k in range(NVAR * NVAR):
                held[i, k, here] = p[k]

        load_p = lambda i: [held[i, k, here] for k in range(NVAR * NVAR)]
        return here, emit, store_p, load_p

    def forward(g, _):
        here, emit, store_p, _ = register(g)
        compose_forward(cells, lambda i, a, b: lower[a, b, i, here], store_p, emit)
        return 0

    def backward(g, _):
        here, emit, _, load_p = register(g)
        compose_backward(cells, lambda i, a, b: upper[a, b, i, here], load_p, emit)
        return 0

    lax.fori_loop(0, rows // ROWS, forward, 0)
    turn()
    lax.fori_loop(0, rows // ROWS, backward, 0)


def compose_y_kernel(lower, upper, y_inverse_hbm, out, y_inverse, held, semaphores):
    load = pltpu.make_async_copy(y_inverse_hbm, y_inverse, semaphores.at[0])
    load.start()
    cells_y = lower.shape[1]

    def emit(which, matrix):
        for a in range(NVAR):
            for b in range(NVAR):
                out[entry(which, a, b)] = matrix[NVAR * a + b]

    def store_p(i, p):
        for k in range(NVAR * NVAR):
            held[i, k] = p[k]

    at = lambda ref: lambda j, a, b: ref[NVAR * a + b, j]
    compose_forward(cells_y, at(lower), store_p, emit)
    compose_backward(
        cells_y, at(upper), lambda i: [held[i, k] for k in range(NVAR * NVAR)], emit
    )
    load.wait()


def local_x_kernel(
    field, forcing, x_pair, x_cross, y_pair, y_cross, inverse, lower, upper, _,
    reduced, source_out, padded, held,
):
    cells, rows, lanes = field.shape[1:]
    zero = jnp.zeros((rows, lanes), F32)
    middle = pl.ds(ROWS, rows)
    for c in range(NVAR):
        for i in range(cells):
            padded[c, i + 2, middle] = field[c, i]

    def y_before(value):
        for c in range(NVAR):
            for k in range(2):
                for i in range(cells):
                    padded[c, i + 2, ROWS - 2 + k] = value(c, k, i)

    def y_after(value):
        for c in range(NVAR):
            for k in range(2):
                for i in range(cells):
                    padded[c, i + 2, ROWS + rows + k] = value(c, k, i)

    def x_before(value):
        for c in range(NVAR):
            for k in range(2):
                padded[c, k, middle] = value(c, k)

    def x_after(value):
        for c in range(NVAR):
            for k in range(2):
                padded[c, cells + 2 + k, middle] = value(c, k)

    for axis, before, behind, pair, cross, empty in (
        ("px", x_before, x_after, lambda *k: x_pair[k], x_cross, jnp.zeros((rows, lanes), F32)),
        ("py", y_before, y_after, lambda *k: y_pair[k], y_cross, jnp.zeros((lanes,), F32)),
    ):
        at, count = lax.axis_index(axis), lax.axis_size(axis)

        @pl.when(bit(axis, 0) == 0)
        def _(before=before, behind=behind, pair=pair, cross=cross):
            before(lambda *k: cross[k])
            behind(pair)

        @pl.when(bit(axis, 0) == 1)
        def _(before=before, behind=behind, pair=pair, cross=cross):
            before(pair)
            behind(lambda *k: cross[k])

        @pl.when(at == 0)
        def _(before=before, empty=empty):
            before(lambda *k: empty)

        @pl.when(at == count - 1)
        def _(behind=behind, empty=empty):
            behind(lambda *k: empty)

    def right_side(i):
        out = []
        for c in range(NVAR):
            centre = padded[c, i + 2, middle]
            along_x = (
                padded[c, i, middle] - 4.0 * padded[c, i + 1, middle] + 6.0 * centre
                - 4.0 * padded[c, i + 3, middle] + padded[c, i + 4, middle]
            )
            along_y = (
                padded[c, i + 2, pl.ds(ROWS - 2, rows)]
                - 4.0 * padded[c, i + 2, pl.ds(ROWS - 1, rows)]
                + 6.0 * centre
                - 4.0 * padded[c, i + 2, pl.ds(ROWS + 1, rows)]
                + padded[c, i + 2, pl.ds(ROWS + 2, rows)]
            )
            out.append(forcing[c, i] - DISSIPATION * (along_x + along_y))
        return out

    def forward(i, v):
        s = matvec(lambda a, b: inverse[a, b, i], right_side(i))
        for c in range(NVAR):
            source_out[c, i] = s[c]
        v = minus(s, matvec(lambda a, b: lower[a, b, i], list(v)))
        for c in range(NVAR):
            held[c, i] = v[c]
        return tuple(v)

    v = lax.fori_loop(0, cells, forward, (zero,) * NVAR, unroll=True)
    for c in range(NVAR):
        reduced[0, c] = v[c]

    def backward(k, w):
        i = cells - 1 - k
        product = matvec(lambda a, b: upper[a, b, i], list(w))
        return tuple(held[c, i] - product[c] for c in range(NVAR))

    w = lax.fori_loop(0, cells, backward, (zero,) * NVAR, unroll=True)
    for c in range(NVAR):
        reduced[1, c] = w[c]


def vec(ref, which):
    return [ref[which, c] for c in range(NVAR)]


def entry(which, a, b):
    return (which * NVAR + a) * NVAR + b


def block(matrices, which, rows=slice(None)):
    return lambda a, b: matrices[entry(which, a, b), rows]


def whole(load):
    return [load(a, b) for a in range(NVAR) for b in range(NVAR)]


def in_order(axis, level, radix, bundles, then):
    place = (lax.axis_index(axis) >> level) & (radix - 1)
    for q in range(radix):

        @pl.when(place == q)
        def _(q=q):
            then(q, [bundles[m ^ q] for m in range(radix)])


def begin_kernel(cells, rows, field_hbm, x_lower_hbm, x_upper_hbm, y_lower_hbm, y_upper_hbm,
                 y_pair, y_cross, x_pair, x_cross, x_out, field, x_lower, x_upper, y_lower, y_upper,
                 held, semaphores):
    loads = [(field_hbm, field), (x_lower_hbm, x_lower), (x_upper_hbm, x_upper)]
    for source, target in ((y_lower_hbm, y_lower), (y_upper_hbm, y_upper)):
        for x in range(cells):
            loads.append((source.at[:, pl.ds(x * rows, rows), :], target.at[:, :, x, :]))
    copies = [
        pltpu.make_async_copy(source, target, semaphores.at[k])
        for k, (source, target) in enumerate(loads)
    ]
    for copy in copies:
        copy.start()
    copies[0].wait()

    def y_layers(out, j):
        for c in range(NVAR):
            for k in range(2):
                out[c, k] = field[c, pl.ds(j + k, cells, stride=rows), :]

    def x_layers(out, i):
        for c in range(NVAR):
            for k in range(2):
                out[c, k] = field[c, pl.ds((i + k) * rows, rows), :]

    @pl.when(bit("py", 0) == 0)
    def _():
        y_layers(y_pair, rows - 2)
        y_layers(y_cross, 0)

    @pl.when(bit("py", 0) == 1)
    def _():
        y_layers(y_pair, 0)
        y_layers(y_cross, rows - 2)

    @pl.when(bit("px", 0) == 0)
    def _():
        x_layers(x_pair, cells - 2)
        x_layers(x_cross, 0)

    @pl.when(bit("px", 0) == 1)
    def _():
        x_layers(x_pair, 0)
        x_layers(x_cross, cells - 2)

    copies[1].wait()
    compose_x(x_lower, x_upper, x_out, held, copies[2].wait)
    for copy in copies[3:]:
        copy.wait()


def grouped(refs, radix):
    return list(zip(refs[:radix], refs[radix : 2 * radix], strict=True))


def inflows(group, f):
    out = [f]
    for matrices, vectors in group:
        a = vec(vectors, 0)
        f = a if f is None else plus(matvec(block(matrices, 0), f), a)
        out.append(f)
    return out


def outflow(stretch, f, b):
    matrices, vectors = stretch
    out = vec(vectors, 1)
    if f is not None:
        out = plus(out, matvec(block(matrices, 2), f))
    if b is not None:
        out = plus(out, matvec(block(matrices, 1), b))
    return out


def join_vectors_kernel(axis, level, radix, last, *refs):
    out = refs[-1]

    def union_a(group):
        return inflows(group, None)[-1]

    def union_c(group):
        f, b = inflows(group[:-1], None), None
        for k in reversed(range(radix)):
            b = outflow(group[k], f[k], b)
        return b

    def then(q, group):
        if not last:
            for which, values in enumerate((union_a(group), union_c(group))):
                for k in range(NVAR):
                    out[which, k] = values[k]
            return

        for side, union in enumerate((union_a, union_c)):

            @pl.when(bit(axis, level + radix.bit_length() - 1) == side)
            def _(union=union):
                for k, value in enumerate(union(group)):
                    out[k] = value

    in_order(axis, level, radix, grouped(refs, radix), then)


def piece_of(axis, k):
    for piece, size in enumerate(PIECES[axis]):
        if k < size:
            return piece, k
        k -= size


def rescaled(matrix, log):
    largest = jnp.maximum(functools.reduce(jnp.maximum, [jnp.abs(q) for q in matrix]), 1.0)
    factor = 1.0 / largest
    return [q * factor for q in matrix], log + jnp.log(largest)


def scaled_union(group, at):
    f = [None, rescaled(whole(at(group[0], 0)), 0.0)]
    for m in group[1:-1]:
        matrix, log = f[-1]
        f.append(rescaled(matmat(at(m, 0), matrix), log))
    matrix, log = f[-1]
    c, log = rescaled(matmat(at(group[-1], 2), matrix), log)
    for k in reversed(range(len(group) - 1)):
        through = matmat(at(group[k], 1), c)
        if k:
            own, own_log = f[k]
            own = matmat(at(group[k], 2), own)
        else:
            own, own_log = whole(at(group[0], 2)), jnp.zeros_like(log)
        top = jnp.maximum(log, own_log)
        left, right = jnp.exp(log - top), jnp.exp(own_log - top)
        c, log = rescaled([p * left + q * right for p, q in zip(through, own)], top)
    return c, log


def join_matrices_kernel(axis, level, radix, last, *refs):
    bundles, outs = refs[:radix], refs[radix:]
    lines = outs[0].shape[-2]

    def then(q, group):
        def register(g, _):
            here = pl.ds(pl.multiple_of(g * ROWS, ROWS), ROWS)
            at = lambda m, which: block(m, which, here)

            def emit(which, matrix):
                for k, value in enumerate(matrix):
                    if last:
                        piece, at_k = piece_of(axis, k)
                        outs[piece][at_k, here] = value
                    else:
                        outs[0][which * NVAR * NVAR + k, here] = value

            if last and axis in SCALED:
                c, log = scaled_union(group, at)
                emit(2, c + [log])
                return 0
            f = [None, whole(at(group[0], 0))]
            for m in group[1:-1]:
                f.append(matmat(at(m, 0), f[-1]))
            if not last:
                emit(0, matmat(at(group[-1], 0), f[-1]))
                r = whole(at(group[-1], 1))
                for m in reversed(group[:-1]):
                    r = matmat(at(m, 1), r)
                emit(1, r)
            c = matmat(at(group[-1], 2), f[-1])
            for k in reversed(range(1, radix - 1)):
                c = plus(matmat(at(group[k], 1), c), matmat(at(group[k], 2), f[k]))
            emit(2, plus(matmat(at(group[0], 1), c), whole(at(group[0], 2))))
            return 0

        lax.fori_loop(0, lines // ROWS, register, 0)

    wanted = bit(axis, level + radix.bit_length() - 1) == 1 if last else True

    @pl.when(wanted)
    def _():
        in_order(axis, level, radix, bundles, then)


def descend(axis, radices, refs, f_ref, b_ref):
    sizes = [2 * r for r in radices[:-1]]
    levels = [sum(r.bit_length() - 1 for r in radices[:t]) for t in range(len(radices))]
    *c_pieces, own, got = refs[sum(sizes) : descend_count(axis, radices)]
    shape = f_ref.shape[1:]

    def got_c(a, b):
        piece, at_k = piece_of(axis, NVAR * a + b)
        return c_pieces[piece][at_k]

    @pl.when(bit(axis, levels[-1]) == 0)
    def _():
        through = matvec(got_c, [own[k] for k in range(NVAR)])
        if axis in SCALED:
            piece, at_k = piece_of(axis, NVAR * NVAR)
            third = jnp.exp(c_pieces[piece][at_k] * (1.0 / 3.0))
            through = [t * third * third * third for t in through]
        for k in range(NVAR):
            f_ref[k] = jnp.zeros(shape, F32)
            b_ref[k] = through[k] + got[k]

    @pl.when(bit(axis, levels[-1]) == 1)
    def _():
        for k in range(NVAR):
            f_ref[k] = got[k]
            b_ref[k] = jnp.zeros(shape, F32)

    for t in reversed(range(len(radices) - 1)):
        radix, first = radices[t], sum(sizes[:t])

        def then(q, group, radix=radix):
            f = inflows(group[:-1], [f_ref[k] for k in range(NVAR)])
            b = [b_ref[k] for k in range(NVAR)]
            for k in reversed(range(q + 1, radix)):
                b = outflow(group[k], f[k], b)
            for k in range(NVAR):
                f_ref[k] = f[q][k]
                b_ref[k] = b[k]

        here = grouped(refs[first : first + sizes[t]], radix)
        in_order(axis, levels[t], radix, here, then)


def descend_count(axis, radices):
    return sum(2 * r for r in radices[:-1]) + len(PIECES[axis]) + 2


def middle_kernel(radices, *rest):
    (source, x_lower, x_upper, y_inverse, y_lower, y_upper,
     reduced, y_source, f_ref, b_ref, held) = rest[descend_count("px", radices) :]
    cells, rows = source.shape[1:3]
    descend("px", radices, rest, f_ref, b_ref)

    def forward(i, v):
        product = matvec(lambda a, b: x_lower[a, b, i], list(v))
        v = [source[c, i] - product[c] for c in range(NVAR)]
        for c in range(NVAR):
            held[c, pl.ds(pl.multiple_of(i * rows, rows), rows)] = v[c]
        return tuple(v)

    lax.fori_loop(0, cells, forward, tuple(f_ref[k] for k in range(NVAR)), unroll=True)

    def backward(k, w):
        i = cells - 1 - k
        here = pl.ds(pl.multiple_of(i * rows, rows), rows)
        product = matvec(lambda a, b: x_upper[a, b, i], list(w))
        w = [held[c, here] - product[c] for c in range(NVAR)]
        s = matvec(lambda a, b: y_inverse[a, b, here], w)
        for c in range(NVAR):
            y_source[c, here] = s[c]
        return tuple(w)

    lax.fori_loop(0, cells, backward, tuple(b_ref[k] for k in range(NVAR)), unroll=True)

    def line(j):
        return pl.ds(j, cells, stride=rows)

    zero = jnp.zeros((cells, source.shape[3]), F32)

    def y_forward(j, v):
        product = matvec(lambda a, b: y_lower[NVAR * a + b, j], list(v))
        v = [y_source[c, line(j), :] - product[c] for c in range(NVAR)]
        for c in range(NVAR):
            held[c, pl.ds(pl.multiple_of(j * cells, cells), cells)] = v[c]
        return tuple(v)

    v = lax.fori_loop(0, rows, y_forward, (zero,) * NVAR, unroll=True)

    def y_backward(k, w):
        j = rows - 1 - k
        product = matvec(lambda a, b: y_upper[NVAR * a + b, j], list(w))
        here = pl.ds(pl.multiple_of(j * cells, cells), cells)
        return tuple(held[c, here] - product[c] for c in range(NVAR))

    w = lax.fori_loop(0, rows, y_backward, (zero,) * NVAR, unroll=True)
    for c in range(NVAR):
        reduced[0, c] = v[c]
        reduced[1, c] = w[c]


def end_kernel(radices, cells, rows, *rest):
    first = descend_count("py", radices)
    y_source, y_lower, y_upper, out, f_ref, b_ref, held = rest[first:]
    descend("py", radices, rest, f_ref, b_ref)

    def line(j):
        return pl.ds(j, cells, stride=rows)

    def forward(j, v):
        product = matvec(lambda a, b: y_lower[NVAR * a + b, j], list(v))
        v = [y_source[c, line(j), :] - product[c] for c in range(NVAR)]
        for c in range(NVAR):
            held[c, pl.ds(pl.multiple_of(j * cells, cells), cells)] = v[c]
        return tuple(v)

    lax.fori_loop(0, rows, forward, tuple(f_ref[k] for k in range(NVAR)), unroll=True)

    def backward(k, w):
        j = rows - 1 - k
        here = pl.ds(pl.multiple_of(j * cells, cells), cells)
        product = matvec(lambda a, b: y_upper[NVAR * a + b, j], list(w))
        w = [held[c, here] - product[c] for c in range(NVAR)]
        for c in range(NVAR):
            out[c, line(j), :] = w[c]
        return tuple(w)

    lax.fori_loop(0, rows, backward, tuple(b_ref[k] for k in range(NVAR)), unroll=True)


def radices_of(count):
    out, rest = [], count // 2
    while rest > 1:
        out.append(4 if rest % 4 == 0 else 2)
        rest //= out[-1]
    return out + [2]


def per_device(field, forcing, x_inverse, x_lower, x_upper, y_inverse, y_lower, y_upper):
    cells, rows, lanes = field.shape[1:]
    x_radices, y_radices = radices_of(lax.axis_size("px")), radices_of(lax.axis_size("py"))

    def swap(value, axis, step):
        pairs = [(i, i ^ step) for i in range(lax.axis_size(axis))]
        return lax.ppermute(value, axis, pairs)

    def across(value, axis):
        n = lax.axis_size(axis)
        pairs = [(i, (i + 1) % n) for i in range(1, n, 2)]
        if axis == "px":
            return lax.ppermute(value, axis, pairs + [(j, i) for i, j in pairs])
        swaps = []
        for x in range(lax.axis_size("px")):
            inner = [(x * n + i, x * n + j) for i, j in pairs[:-1]]
            swaps += inner + [(j, i) for i, j in inner]
            swaps += [(x * n + i, (x ^ 1) * n + i) for i in (0, n - 1)]
        return lax.ppermute(value, ("px", "py"), swaps)

    flat = lambda m: m.reshape(m.shape[:-3] + (cells * rows, lanes))
    y_inverse = flat(y_inverse)

    every = NVAR * NVAR
    y_pair, y_cross, x_pair, x_cross, x_m, field, x_lower, x_upper, y_lower, y_upper = call(
        functools.partial(begin_kernel, cells, rows), "begin",
        [(NVAR, 2, cells, lanes)] * 2 + [(NVAR, 2, rows, lanes), (NVAR, 6, rows, lanes)]
        + [(MATRICES, rows, lanes), (NVAR, cells * rows, lanes)] + [x_lower.shape] * 2
        + [(every, rows, cells, lanes)] * 2,
        [], [(cells, every, rows, lanes)],
        from_hbm=[flat(field), x_lower, x_upper]
        + [m.reshape(every, cells * rows, lanes) for m in (y_lower, y_upper)],
        copies=3 + 2 * cells,
    )
    field = field.reshape(NVAR, cells, rows, lanes)
    y_cross, x_cross = across(y_cross, "py"), across(x_cross, "px")
    y_pair, x_pair = swap(y_pair, "py", 1), swap(x_pair, "px", 1)
    halos = (x_pair, x_cross, y_pair, y_cross)

    def exchange(axis, radices, own_m, got_m, own_v, rest):
        operands, level = [], 0
        for t, radix in enumerate(radices[:-1]):
            last = t == len(radices) - 2
            settings = (axis, level, radix, last)
            got_v = [swap(own_v, axis, k << level) for k in range(1, radix)]
            lines = own_m.shape[1:]
            sizes = PIECES[axis] if last else (MATRICES,)
            next_m = call(functools.partial(join_matrices_kernel, *settings), "join_matrices",
                          [(size, *lines) for size in sizes], [own_m, *got_m])
            next_m = list(next_m) if len(sizes) > 1 else [next_m]
            next_level = level + radix.bit_length() - 1
            next_got = [swap(m, axis, k << next_level)
                        for k in range(1, radices[t + 1]) for m in next_m]
            count = len(operands)
            operands += [own_m, *got_m, own_v, *got_v]
            held = hold(operands + rest)
            operands, rest = held[: len(operands)], held[len(operands) :]
            own_v = call(functools.partial(join_vectors_kernel, *settings), "join_vectors",
                         [own_v.shape[last:]], operands[count:])
            if not last:
                next_got = hold(next_got, own_v)
            own_m, got_m, level = next_m[0], next_got, next_level
        operands += [*got_m, own_v, swap(own_v, axis, 1 << level)]
        held = hold(operands + rest)
        return held[: len(operands)], held[len(operands) :]

    y_m, y_inverse = call(
        compose_y_kernel, "compose_y", [(MATRICES, cells, lanes), y_inverse.shape],
        [y_lower, y_upper], [(rows, every, cells, lanes)], from_hbm=[y_inverse], copies=1,
    )
    y_got = [swap(y_m, "py", k) for k in range(1, y_radices[0])]
    reduced, source = call(
        local_x_kernel, "local_x",
        [(VX, NVAR, rows, lanes), (NVAR, cells, rows, lanes)],
        [field, forcing, *halos, x_inverse, x_lower, x_upper, y_m],
        [(NVAR, cells + 4, rows + 2 * ROWS, lanes), (NVAR, cells, rows, lanes)],
    )
    x_got = [swap(x_m, "px", k) for k in range(1, x_radices[0])]
    rest = [source, x_lower, x_upper, y_inverse, y_lower, y_upper]
    operands, rest = exchange("px", x_radices, x_m, x_got, reduced, rest)
    reduced, source = call(
        functools.partial(middle_kernel, x_radices), "middle",
        [(2, NVAR, cells, lanes), (NVAR, cells * rows, lanes)],
        operands + rest,
        [(NVAR, rows, lanes), (NVAR, rows, lanes), (NVAR, cells * rows, lanes)],
    )
    y_m, *y_got = hold([y_m, *y_got], reduced)
    operands, rest = exchange(
        "py", y_radices, y_m, y_got, reduced, [source, *rest[-2:]]
    )
    out = call(
        functools.partial(end_kernel, y_radices, cells, rows), "end",
        [(NVAR, cells * rows, lanes)],
        operands + rest,
        [(NVAR, cells, lanes), (NVAR, cells, lanes), (NVAR, cells * rows, lanes)],
        result_in_hbm=True,
    )
    return out.reshape(NVAR, cells, rows, lanes)


def solution(mesh):
    cell = P(None, "px", "py", None)
    blocks = P(None, None, "px", "py", None)
    return jax.shard_map(
        per_device,
        mesh=mesh,
        in_specs=(cell, cell) + (blocks,) * 6,
        out_specs=cell,
        check_vma=False,
    )
```

```python
import functools

import jax
import jax.numpy as jnp
from jax import lax
from jax.experimental import pallas as pl
from jax.experimental.pallas import tpu as pltpu
from jax.sharding import PartitionSpec as P

DISSIPATION = 0.1
NVAR = 5
F32 = jnp.float32
ROWS = 8
UNROLL = 3
MATRICES = 3 * NVAR * NVAR
VX = 2
SCALED = ("py",)
PIECES = {"px": (25,), "py": (13, 13)}
VMEM_BYTES = 12 * 1024 * 1024


def call(kernel, name, out_shapes, operands, scratch=(), result_in_hbm=False, from_hbm=(),
         copies=0):
    vmem = pl.BlockSpec(memory_space=pltpu.VMEM)
    make = jax.ShapeDtypeStruct if result_in_hbm else pltpu.VMEM
    shapes = [make(s, F32) for s in out_shapes]
    single = len(shapes) == 1
    operands = [pltpu.with_memory_space_constraint(x, pltpu.VMEM) for x in operands]
    outer = [pltpu.with_memory_space_constraint(x, pltpu.HBM) for x in from_hbm]
    semaphores = [pltpu.SemaphoreType.DMA((copies,))] if copies else []
    return pl.pallas_call(
        kernel,
        name=name,
        out_shape=shapes[0] if single else shapes,
        in_specs=[vmem] * len(operands) + [pl.BlockSpec(memory_space=pltpu.HBM)] * len(outer),
        out_specs=vmem if single else [vmem] * len(shapes),
        scratch_shapes=[pltpu.VMEM(s, F32) for s in scratch] + semaphores,
        compiler_params=pltpu.CompilerParams(vmem_limit_bytes=VMEM_BYTES),
    )(*operands, *outer)


def hold(arrays, *others):
    def nothing(*refs):
        pass

    operands = [pltpu.with_memory_space_constraint(x, pltpu.VMEM) for x in (*arrays, *others)]
    anywhere = pl.BlockSpec(memory_space=pl.ANY)
    held = pl.pallas_call(
        nothing,
        name="hold",
        out_shape=[pltpu.VMEM(x.shape, F32) for x in arrays],
        in_specs=[anywhere] * len(operands),
        out_specs=[anywhere] * len(arrays),
        input_output_aliases={k: k for k in range(len(arrays))},
        compiler_params=pltpu.CompilerParams(vmem_limit_bytes=1024 * 1024),
    )(*operands)
    return list(held)


def bit(axis, level):
    return (lax.axis_index(axis) >> level) & 1


def tree(terms):
    while len(terms) > 1:
        pairs = [terms[k] + terms[k + 1] for k in range(0, len(terms) - 1, 2)]
        terms = pairs + (terms[-1:] if len(terms) % 2 else [])
    return terms[0]


def matvec(load, vector):
    return [tree([load(a, b) * vector[b] for b in range(NVAR)]) for a in range(NVAR)]


def matmat(load, matrix):
    out = []
    for a in range(NVAR):
        row = [load(a, b) for b in range(NVAR)]
        for c in range(NVAR):
            out.append(tree([row[b] * matrix[NVAR * b + c] for b in range(NVAR)]))
    return out


def plus(left, right):
    return [p + q for p, q in zip(left, right, strict=True)]


def minus(left, right):
    return [p - q for p, q in zip(left, right, strict=True)]


def signed(matrix, length):
    return [-q for q in matrix] if length % 2 else list(matrix)


def compose_forward(length, lower_at, store_p, emit):
    first = whole(lambda a, b: lower_at(0, a, b))
    store_p(0, first)

    def forward(i, p):
        p = matmat(lambda a, b: lower_at(i, a, b), p)
        store_p(i, p)
        return tuple(p)

    last = lax.fori_loop(1, length, forward, tuple(first), unroll=UNROLL)
    emit(0, signed(last, length))


def compose_backward(length, upper_at, load_p, emit, keep=lambda i, w, r: None):
    def backward(k, carried):
        w, r = carried
        i = length - 1 - k
        here = whole(lambda a, b: upper_at(i, a, b))
        at = lambda a, b: here[NVAR * a + b]
        w, r = tuple(plus(load_p(i), matmat(at, w))), tuple(matmat(at, r))
        keep(i, w, r)
        return w, r

    w = tuple(load_p(length - 1))
    r = tuple(whole(lambda a, b: upper_at(length - 1, a, b)))
    keep(length - 1, w, r)
    w, r = lax.fori_loop(1, length, backward, (w, r), unroll=UNROLL)
    emit(1, signed(r, length))
    emit(2, [-q for q in w])


def compose_x(lower, upper, out, held, turn):
    cells, rows = lower.shape[2:4]

    def register(g):
        here = pl.ds(pl.multiple_of(g * ROWS, ROWS), ROWS)

        def emit(which, matrix):
            for k, value in enumerate(matrix):
                out[which * NVAR * NVAR + k, here] = value

        def store_p(i, p):
            for k in range(NVAR * NVAR):
                held[i, k, here] = p[k]

        load_p = lambda i: [held[i, k, here] for k in range(NVAR * NVAR)]
        return here, emit, store_p, load_p

    def forward(g, _):
        here, emit, store_p, _ = register(g)
        compose_forward(cells, lambda i, a, b: lower[a, b, i, here], store_p, emit)
        return 0

    def backward(g, _):
        here, emit, _, load_p = register(g)
        compose_backward(cells, lambda i, a, b: upper[a, b, i, here], load_p, emit)
        return 0

    lax.fori_loop(0, rows // ROWS, forward, 0)
    turn()
    lax.fori_loop(0, rows // ROWS, backward, 0)


def compose_y_kernel(lower, upper, y_inverse_hbm, out, y_inverse, held, semaphores):
    load = pltpu.make_async_copy(y_inverse_hbm, y_inverse, semaphores.at[0])
    load.start()
    cells_y = lower.shape[1]

    def emit(which, matrix):
        for a in range(NVAR):
            for b in range(NVAR):
                out[entry(which, a, b)] = matrix[NVAR * a + b]

    def store_p(i, p):
        for k in range(NVAR * NVAR):
            held[i, k] = p[k]

    at = lambda ref: lambda j, a, b: ref[NVAR * a + b, j]
    compose_forward(cells_y, at(lower), store_p, emit)
    compose_backward(
        cells_y, at(upper), lambda i: [held[i, k] for k in range(NVAR * NVAR)], emit
    )
    load.wait()


def responses_kernel(lower, upper, _, from_f, from_b, held):
    def store_p(i, p):
        for k in range(NVAR * NVAR):
            held[i, k] = p[k]

    def keep(j, w, r):
        for k in range(NVAR * NVAR):
            from_f[j, k] = w[k]
            from_b[j, k] = r[k]

    at = lambda ref: lambda j, a, b: ref[NVAR * a + b, j]
    load_p = lambda i: [held[i, k] for k in range(NVAR * NVAR)]
    nothing = lambda which, matrix: None
    compose_forward(lower.shape[1], at(lower), store_p, nothing)
    compose_backward(lower.shape[1], at(upper), load_p, nothing, keep)


def local_x_kernel(
    field, forcing, x_pair, x_cross, y_pair, y_cross, inverse, lower, upper, _,
    reduced, source_out, padded, held,
):
    cells, rows, lanes = field.shape[1:]
    zero = jnp.zeros((rows, lanes), F32)
    middle = pl.ds(ROWS, rows)
    for c in range(NVAR):
        for i in range(cells):
            padded[c, i + 2, middle] = field[c, i]

    def y_before(value):
        for c in range(NVAR):
            for k in range(2):
                for i in range(cells):
                    padded[c, i + 2, ROWS - 2 + k] = value(c, k, i)

    def y_after(value):
        for c in range(NVAR):
            for k in range(2):
                for i in range(cells):
                    padded[c, i + 2, ROWS + rows + k] = value(c, k, i)

    def x_before(value):
        for c in range(NVAR):
            for k in range(2):
                padded[c, k, middle] = value(c, k)

    def x_after(value):
        for c in range(NVAR):
            for k in range(2):
                padded[c, cells + 2 + k, middle] = value(c, k)

    for axis, before, behind, pair, cross, empty in (
        ("px", x_before, x_after, lambda *k: x_pair[k], x_cross, jnp.zeros((rows, lanes), F32)),
        ("py", y_before, y_after, lambda *k: y_pair[k], y_cross, jnp.zeros((lanes,), F32)),
    ):
        at, count = lax.axis_index(axis), lax.axis_size(axis)

        @pl.when(bit(axis, 0) == 0)
        def _(before=before, behind=behind, pair=pair, cross=cross):
            before(lambda *k: cross[k])
            behind(pair)

        @pl.when(bit(axis, 0) == 1)
        def _(before=before, behind=behind, pair=pair, cross=cross):
            before(pair)
            behind(lambda *k: cross[k])

        @pl.when(at == 0)
        def _(before=before, empty=empty):
            before(lambda *k: empty)

        @pl.when(at == count - 1)
        def _(behind=behind, empty=empty):
            behind(lambda *k: empty)

    def right_side(i):
        out = []
        for c in range(NVAR):
            centre = padded[c, i + 2, middle]
            along_x = (
                padded[c, i, middle] - 4.0 * padded[c, i + 1, middle] + 6.0 * centre
                - 4.0 * padded[c, i + 3, middle] + padded[c, i + 4, middle]
            )
            along_y = (
                padded[c, i + 2, pl.ds(ROWS - 2, rows)]
                - 4.0 * padded[c, i + 2, pl.ds(ROWS - 1, rows)]
                + 6.0 * centre
                - 4.0 * padded[c, i + 2, pl.ds(ROWS + 1, rows)]
                + padded[c, i + 2, pl.ds(ROWS + 2, rows)]
            )
            out.append(forcing[c, i] - DISSIPATION * (along_x + along_y))
        return out

    def forward(i, v):
        s = matvec(lambda a, b: inverse[a, b, i], right_side(i))
        for c in range(NVAR):
            source_out[c, i] = s[c]
        v = minus(s, matvec(lambda a, b: lower[a, b, i], list(v)))
        for c in range(NVAR):
            held[c, i] = v[c]
        return tuple(v)

    v = lax.fori_loop(0, cells, forward, (zero,) * NVAR, unroll=True)
    for c in range(NVAR):
        reduced[0, c] = v[c]

    def backward(k, w):
        i = cells - 1 - k
        product = matvec(lambda a, b: upper[a, b, i], list(w))
        return tuple(held[c, i] - product[c] for c in range(NVAR))

    w = lax.fori_loop(0, cells, backward, (zero,) * NVAR, unroll=True)
    for c in range(NVAR):
        reduced[1, c] = w[c]


def vec(ref, which):
    return [ref[which, c] for c in range(NVAR)]


def entry(which, a, b):
    return (which * NVAR + a) * NVAR + b


def block(matrices, which, rows=slice(None)):
    return lambda a, b: matrices[entry(which, a, b), rows]


def whole(load):
    return [load(a, b) for a in range(NVAR) for b in range(NVAR)]


def in_order(axis, level, radix, bundles, then):
    place = (lax.axis_index(axis) >> level) & (radix - 1)
    for q in range(radix):

        @pl.when(place == q)
        def _(q=q):
            then(q, [bundles[m ^ q] for m in range(radix)])


def begin_kernel(cells, rows, field_hbm, x_lower_hbm, x_upper_hbm, y_lower_hbm, y_upper_hbm,
                 y_pair, y_cross, x_pair, x_cross, x_out, field, x_lower, x_upper, y_lower, y_upper,
                 held, semaphores):
    loads = [(field_hbm, field), (x_lower_hbm, x_lower), (x_upper_hbm, x_upper)]
    for source, target in ((y_lower_hbm, y_lower), (y_upper_hbm, y_upper)):
        for x in range(cells):
            loads.append((source.at[:, pl.ds(x * rows, rows), :], target.at[:, :, x, :]))
    copies = [
        pltpu.make_async_copy(source, target, semaphores.at[k])
        for k, (source, target) in enumerate(loads)
    ]
    for copy in copies:
        copy.start()
    copies[0].wait()

    def y_layers(out, j):
        for c in range(NVAR):
            for k in range(2):
                out[c, k] = field[c, pl.ds(j + k, cells, stride=rows), :]

    def x_layers(out, i):
        for c in range(NVAR):
            for k in range(2):
                out[c, k] = field[c, pl.ds((i + k) * rows, rows), :]

    @pl.when(bit("py", 0) == 0)
    def _():
        y_layers(y_pair, rows - 2)
        y_layers(y_cross, 0)

    @pl.when(bit("py", 0) == 1)
    def _():
        y_layers(y_pair, 0)
        y_layers(y_cross, rows - 2)

    @pl.when(bit("px", 0) == 0)
    def _():
        x_layers(x_pair, cells - 2)
        x_layers(x_cross, 0)

    @pl.when(bit("px", 0) == 1)
    def _():
        x_layers(x_pair, 0)
        x_layers(x_cross, cells - 2)

    copies[1].wait()
    compose_x(x_lower, x_upper, x_out, held, copies[2].wait)
    for copy in copies[3:]:
        copy.wait()


def grouped(refs, radix):
    return list(zip(refs[:radix], refs[radix : 2 * radix], strict=True))


def inflows(group, f):
    out = [f]
    for matrices, vectors in group:
        a = vec(vectors, 0)
        f = a if f is None else plus(matvec(block(matrices, 0), f), a)
        out.append(f)
    return out


def outflow(stretch, f, b):
    matrices, vectors = stretch
    out = vec(vectors, 1)
    if f is not None:
        out = plus(out, matvec(block(matrices, 2), f))
    if b is not None:
        out = plus(out, matvec(block(matrices, 1), b))
    return out


def join_vectors_kernel(axis, level, radix, last, *refs):
    out = refs[-1]

    def union_a(group):
        return inflows(group, None)[-1]

    def union_c(group):
        f, b = inflows(group[:-1], None), None
        for k in reversed(range(radix)):
            b = outflow(group[k], f[k], b)
        return b

    def then(q, group):
        if not last:
            for which, values in enumerate((union_a(group), union_c(group))):
                for k in range(NVAR):
                    out[which, k] = values[k]
            return

        for side, union in enumerate((union_a, union_c)):

            @pl.when(bit(axis, level + radix.bit_length() - 1) == side)
            def _(union=union):
                for k, value in enumerate(union(group)):
                    out[k] = value

    in_order(axis, level, radix, grouped(refs, radix), then)


def piece_of(axis, k):
    for piece, size in enumerate(PIECES[axis]):
        if k < size:
            return piece, k
        k -= size


def rescaled(matrix, log):
    largest = jnp.maximum(functools.reduce(jnp.maximum, [jnp.abs(q) for q in matrix]), 1.0)
    factor = 1.0 / largest
    return [q * factor for q in matrix], log + jnp.log(largest)


def scaled_union(group, at):
    f = [None, rescaled(whole(at(group[0], 0)), 0.0)]
    for m in group[1:-1]:
        matrix, log = f[-1]
        f.append(rescaled(matmat(at(m, 0), matrix), log))
    matrix, log = f[-1]
    c, log = rescaled(matmat(at(group[-1], 2), matrix), log)
    for k in reversed(range(len(group) - 1)):
        through = matmat(at(group[k], 1), c)
        if k:
            own, own_log = f[k]
            own = matmat(at(group[k], 2), own)
        else:
            own, own_log = whole(at(group[0], 2)), jnp.zeros_like(log)
        top = jnp.maximum(log, own_log)
        left, right = jnp.exp(log - top), jnp.exp(own_log - top)
        c, log = rescaled([p * left + q * right for p, q in zip(through, own)], top)
    return c, log


def join_matrices_kernel(axis, level, radix, last, *refs):
    bundles, outs = refs[:radix], refs[radix:]
    lines = outs[0].shape[-2]

    def then(q, group):
        def register(g, _):
            here = pl.ds(pl.multiple_of(g * ROWS, ROWS), ROWS)
            at = lambda m, which: block(m, which, here)

            def emit(which, matrix):
                for k, value in enumerate(matrix):
                    if last:
                        piece, at_k = piece_of(axis, k)
                        outs[piece][at_k, here] = value
                    else:
                        outs[0][which * NVAR * NVAR + k, here] = value

            if last and axis in SCALED:
                c, log = scaled_union(group, at)
                emit(2, c + [log])
                return 0
            f = [None, whole(at(group[0], 0))]
            for m in group[1:-1]:
                f.append(matmat(at(m, 0), f[-1]))
            if not last:
                emit(0, matmat(at(group[-1], 0), f[-1]))
                r = whole(at(group[-1], 1))
                for m in reversed(group[:-1]):
                    r = matmat(at(m, 1), r)
                emit(1, r)
            c = matmat(at(group[-1], 2), f[-1])
            for k in reversed(range(1, radix - 1)):
                c = plus(matmat(at(group[k], 1), c), matmat(at(group[k], 2), f[k]))
            emit(2, plus(matmat(at(group[0], 1), c), whole(at(group[0], 2))))
            return 0

        lax.fori_loop(0, lines // ROWS, register, 0)

    wanted = bit(axis, level + radix.bit_length() - 1) == 1 if last else True

    @pl.when(wanted)
    def _():
        in_order(axis, level, radix, bundles, then)


def descend(axis, radices, refs, f_ref, b_ref):
    sizes = [2 * r for r in radices[:-1]]
    levels = [sum(r.bit_length() - 1 for r in radices[:t]) for t in range(len(radices))]
    *c_pieces, own, got = refs[sum(sizes) : descend_count(axis, radices)]
    shape = f_ref.shape[1:]

    def got_c(a, b):
        piece, at_k = piece_of(axis, NVAR * a + b)
        return c_pieces[piece][at_k]

    @pl.when(bit(axis, levels[-1]) == 0)
    def _():
        through = matvec(got_c, [own[k] for k in range(NVAR)])
        if axis in SCALED:
            piece, at_k = piece_of(axis, NVAR * NVAR)
            third = jnp.exp(c_pieces[piece][at_k] * (1.0 / 3.0))
            through = [t * third * third * third for t in through]
        for k in range(NVAR):
            f_ref[k] = jnp.zeros(shape, F32)
            b_ref[k] = through[k] + got[k]

    @pl.when(bit(axis, levels[-1]) == 1)
    def _():
        for k in range(NVAR):
            f_ref[k] = got[k]
            b_ref[k] = jnp.zeros(shape, F32)

    for t in reversed(range(len(radices) - 1)):
        radix, first = radices[t], sum(sizes[:t])

        def then(q, group, radix=radix):
            f = inflows(group[:-1], [f_ref[k] for k in range(NVAR)])
            b = [b_ref[k] for k in range(NVAR)]
            for k in reversed(range(q + 1, radix)):
                b = outflow(group[k], f[k], b)
            for k in range(NVAR):
                f_ref[k] = f[q][k]
                b_ref[k] = b[k]

        here = grouped(refs[first : first + sizes[t]], radix)
        in_order(axis, levels[t], radix, here, then)


def descend_count(axis, radices):
    return sum(2 * r for r in radices[:-1]) + len(PIECES[axis]) + 2


def middle_kernel(radices, *rest):
    (source, x_lower, x_upper, y_inverse, y_lower, y_upper,
     reduced, y_cells, f_ref, b_ref, held, y_source) = rest[descend_count("px", radices) :]
    cells, rows = source.shape[1:3]
    descend("px", radices, rest, f_ref, b_ref)

    def forward(i, v):
        product = matvec(lambda a, b: x_lower[a, b, i], list(v))
        v = [source[c, i] - product[c] for c in range(NVAR)]
        for c in range(NVAR):
            held[c, pl.ds(pl.multiple_of(i * rows, rows), rows)] = v[c]
        return tuple(v)

    lax.fori_loop(0, cells, forward, tuple(f_ref[k] for k in range(NVAR)), unroll=True)

    def backward(k, w):
        i = cells - 1 - k
        here = pl.ds(pl.multiple_of(i * rows, rows), rows)
        product = matvec(lambda a, b: x_upper[a, b, i], list(w))
        w = [held[c, here] - product[c] for c in range(NVAR)]
        s = matvec(lambda a, b: y_inverse[a, b, here], w)
        for c in range(NVAR):
            y_source[c, here] = s[c]
        return tuple(w)

    lax.fori_loop(0, cells, backward, tuple(b_ref[k] for k in range(NVAR)), unroll=True)

    def line(j):
        return pl.ds(j, cells, stride=rows)

    zero = jnp.zeros((cells, source.shape[3]), F32)

    def y_forward(j, v):
        product = matvec(lambda a, b: y_lower[NVAR * a + b, j], list(v))
        v = [y_source[c, line(j), :] - product[c] for c in range(NVAR)]
        for c in range(NVAR):
            held[c, pl.ds(pl.multiple_of(j * cells, cells), cells)] = v[c]
        return tuple(v)

    v = lax.fori_loop(0, rows, y_forward, (zero,) * NVAR, unroll=True)

    def y_backward(k, w):
        j = rows - 1 - k
        product = matvec(lambda a, b: y_upper[NVAR * a + b, j], list(w))
        here = pl.ds(pl.multiple_of(j * cells, cells), cells)
        w = [held[c, here] - product[c] for c in range(NVAR)]
        for c in range(NVAR):
            y_cells[c, here] = w[c]
        return tuple(w)

    w = lax.fori_loop(0, rows, y_backward, (zero,) * NVAR, unroll=True)
    for c in range(NVAR):
        reduced[0, c] = v[c]
        reduced[1, c] = w[c]


def end_kernel(radices, cells, rows, *rest):
    first = descend_count("py", radices)
    y_cells, from_f, from_b, out, f_ref, b_ref = rest[first:]
    descend("py", radices, rest, f_ref, b_ref)
    f = [f_ref[k] for k in range(NVAR)]
    b = [b_ref[k] for k in range(NVAR)]
    for j in range(rows):
        forward = matvec(lambda a, c: from_f[j, NVAR * a + c], f)
        backward = matvec(lambda a, c: from_b[j, NVAR * a + c], b)
        for c in range(NVAR):
            value = y_cells[c, j * cells : (j + 1) * cells]
            value = value + forward[c] if j % 2 else value - forward[c]
            value = value - backward[c] if (rows - j) % 2 else value + backward[c]
            out[c, pl.ds(j, cells, stride=rows), :] = value


def radices_of(count):
    out, rest = [], count // 2
    while rest > 1:
        out.append(4 if rest % 4 == 0 else 2)
        rest //= out[-1]
    return out + [2]


def per_device(field, forcing, x_inverse, x_lower, x_upper, y_inverse, y_lower, y_upper):
    cells, rows, lanes = field.shape[1:]
    x_radices, y_radices = radices_of(lax.axis_size("px")), radices_of(lax.axis_size("py"))

    def swap(value, axis, step):
        pairs = [(i, i ^ step) for i in range(lax.axis_size(axis))]
        return lax.ppermute(value, axis, pairs)

    def across(value, axis):
        n = lax.axis_size(axis)
        pairs = [(i, (i + 1) % n) for i in range(1, n, 2)]
        if axis == "px":
            return lax.ppermute(value, axis, pairs + [(j, i) for i, j in pairs])
        swaps = []
        for x in range(lax.axis_size("px")):
            inner = [(x * n + i, x * n + j) for i, j in pairs[:-1]]
            swaps += inner + [(j, i) for i, j in inner]
            swaps += [(x * n + i, (x ^ 1) * n + i) for i in (0, n - 1)]
        return lax.ppermute(value, ("px", "py"), swaps)

    flat = lambda m: m.reshape(m.shape[:-3] + (cells * rows, lanes))
    y_inverse = flat(y_inverse)

    every = NVAR * NVAR
    y_pair, y_cross, x_pair, x_cross, x_m, field, x_lower, x_upper, y_lower, y_upper = call(
        functools.partial(begin_kernel, cells, rows), "begin",
        [(NVAR, 2, cells, lanes)] * 2 + [(NVAR, 2, rows, lanes), (NVAR, 6, rows, lanes)]
        + [(MATRICES, rows, lanes), (NVAR, cells * rows, lanes)] + [x_lower.shape] * 2
        + [(every, rows, cells, lanes)] * 2,
        [], [(cells, every, rows, lanes)],
        from_hbm=[flat(field), x_lower, x_upper]
        + [m.reshape(every, cells * rows, lanes) for m in (y_lower, y_upper)],
        copies=3 + 2 * cells,
    )
    field = field.reshape(NVAR, cells, rows, lanes)
    y_cross, x_cross = across(y_cross, "py"), across(x_cross, "px")
    y_pair, x_pair = swap(y_pair, "py", 1), swap(x_pair, "px", 1)
    halos = (x_pair, x_cross, y_pair, y_cross)

    def exchange(axis, radices, own_m, got_m, own_v, rest, late=None):
        operands, level = [], 0
        for t, radix in enumerate(radices[:-1]):
            last = t == len(radices) - 2
            settings = (axis, level, radix, last)
            got_v = [swap(own_v, axis, k << level) for k in range(1, radix)]
            lines = own_m.shape[1:]
            sizes = PIECES[axis] if last else (MATRICES,)
            next_m = call(functools.partial(join_matrices_kernel, *settings), "join_matrices",
                          [(size, *lines) for size in sizes], [own_m, *got_m])
            next_m = list(next_m) if len(sizes) > 1 else [next_m]
            next_level = level + radix.bit_length() - 1
            next_got = [swap(m, axis, k << next_level)
                        for k in range(1, radices[t + 1]) for m in next_m]
            count = len(operands)
            operands += [own_m, *got_m, own_v, *got_v]
            held = hold(operands + rest)
            operands, rest = held[: len(operands)], held[len(operands) :]
            own_v = call(functools.partial(join_vectors_kernel, *settings), "join_vectors",
                         [own_v.shape[last:]], operands[count:])
            if not last:
                next_got = hold(next_got, own_v)
            own_m, got_m, level = next_m[0], next_got, next_level
        operands += [*got_m, own_v, swap(own_v, axis, 1 << level)]
        rest = late(own_v, rest) if late else rest
        held = hold(operands + rest)
        return held[: len(operands)], held[len(operands) :]

    y_m, y_inverse = call(
        compose_y_kernel, "compose_y", [(MATRICES, cells, lanes), y_inverse.shape],
        [y_lower, y_upper], [(rows, every, cells, lanes)], from_hbm=[y_inverse], copies=1,
    )
    y_got = [swap(y_m, "py", k) for k in range(1, y_radices[0])]
    reduced, source = call(
        local_x_kernel, "local_x",
        [(VX, NVAR, rows, lanes), (NVAR, cells, rows, lanes)],
        [field, forcing, *halos, x_inverse, x_lower, x_upper, y_m],
        [(NVAR, cells + 4, rows + 2 * ROWS, lanes), (NVAR, cells, rows, lanes)],
    )
    x_got = [swap(x_m, "px", k) for k in range(1, x_radices[0])]
    rest = [source, x_lower, x_upper, y_inverse, y_lower, y_upper]
    operands, rest = exchange("px", x_radices, x_m, x_got, reduced, rest)
    reduced, y_cells = call(
        functools.partial(middle_kernel, x_radices), "middle",
        [(2, NVAR, cells, lanes), (NVAR, cells * rows, lanes)],
        operands + rest,
        [(NVAR, rows, lanes), (NVAR, rows, lanes), (NVAR, cells * rows, lanes),
         (NVAR, cells * rows, lanes)],
    )
    def responses(own_v, rest):
        kept = call(responses_kernel, "responses", [(rows, every, cells, lanes)] * 2,
                    [*rest[1:], own_v], [(rows, every, cells, lanes)])
        return [rest[0], *kept]

    y_m, *y_got = hold([y_m, *y_got], reduced)
    operands, rest = exchange(
        "py", y_radices, y_m, y_got, reduced, [y_cells, *rest[-2:]], responses
    )
    out = call(
        functools.partial(end_kernel, y_radices, cells, rows), "end",
        [(NVAR, cells * rows, lanes)],
        operands + rest,
        [(NVAR, cells, lanes), (NVAR, cells, lanes)],
        result_in_hbm=True,
    )
    return out.reshape(NVAR, cells, rows, lanes)


def solution(mesh):
    cell = P(None, "px", "py", None)
    blocks = P(None, None, "px", "py", None)
    return jax.shard_map(
        per_device,
        mesh=mesh,
        in_specs=(cell, cell) + (blocks,) * 6,
        out_specs=cell,
        check_vma=False,
    )
```
